256 devices in a mesh: row: 32 (over y, z), col: 8 (over x, core).
Axes of the slice: x: 4, y: 4, z: 8, core: 2. Of those that a mesh axis runs over, the one named last changes fastest.
Arguments:
- panel: bfloat16 [131072, 2048], P('row'), as said below
- rhs: float32 [131072, 2048], P('row', 'col'), may hold values from -6 to 6
- block_slot: int32 [128], replicated, may hold values from 0 to 127, each once
- target: float32 [2, 1024], P(None, 'col'), may hold values from -0.125 to 0.125
Outputs:
- solved_rhs: float32 [131072, 2048], P('row', 'col')
- mean_part: float32 [2048], P('col')
The draws below stay inside these ranges and needn't reach their ends.
Inputs may be any that keep to these rules, and one draw needn't show every extreme that they name: block_slot is a permutation of the storage slots. Within every tile of panel the diagonal entries lie between 1 and 3.
All inputs are finite; a program needn't handle non-finite values.
Results may differ from the reference program's by a relative error of at most 0.0034.
Values may be sent and summed in bfloat16 or wider, within the bound.
A program may use at most 128 MiB of HBM per device.

```python
import jax
import jax.numpy as jnp
from jax import lax

B = 1024
NRHS = 2048
NBLK = 128
NTOT = 131072


def draw_panel(key, part):
    key = jax.random.fold_in(key, 11)
    key_off = jax.random.fold_in(key, 1)
    key_diag = jax.random.fold_in(key, 2)
    shape = (NTOT, 2 * B)
    spread = 0.4 / B ** 0.5
    off = jax.random.normal(key_off, shape, jnp.float32) * spread
    dominant = jax.random.uniform(key_diag, shape, jnp.float32, 1.0, 2.0)
    rows = lax_rows(shape)
    cols = lax_cols(shape)
    return jnp.where(rows == cols, dominant, off).astype(jnp.bfloat16)


def lax_rows(shape):
    return jnp.arange(shape[0], dtype=jnp.int32)[:, None] % B


def lax_cols(shape):
    return jnp.arange(shape[1], dtype=jnp.int32)[None, :] % B


def shard_levels(key, shape, cuts, least, largest):
    factor_of, own = 1.0, jax.random.fold_in(key, 6)
    for dim, blocks in cuts:
        draws = jnp.exp(jax.random.uniform(jax.random.fold_in(own, dim), (blocks,), jnp.float32, least / len(cuts), largest / len(cuts)))
        factor_of = factor_of * jnp.repeat(draws, shape[dim] // blocks).reshape([-1 if axis == dim else 1 for axis in range(len(shape))])
    return factor_of


def bell_draw(own_key, extent, scale, most, shards=(), held_as=jnp.bfloat16):
    level = shard_levels(own_key, extent, shards, -0.22, 0.18) if shards else 1.0
    values = jax.random.normal(own_key, extent, jnp.float32) * scale * level
    return jnp.minimum(jnp.maximum(values, -most), most).astype(held_as)


def setup_inputs(seed: int = 0) -> dict:
    key_of = jax.random.split(jax.random.key(seed), 5)
    return {
        "panel": draw_panel(jax.random.fold_in(key_of[4], 71), 0),
        "rhs": bell_draw(key_of[1], (NTOT, NRHS), 1.0, 6.0, ((0, 32), (1, 8)), jnp.float32),
        "block_slot": jax.random.permutation(key_of[2], NBLK).astype(jnp.int32),
        "target": bell_draw(key_of[3], (2, B), (2 * B) ** -0.5, 0.125, ((1, 8),), jnp.float32),
    }


def reference(panel, rhs, block_slot, target):
    count = block_slot.shape[0]
    order = jnp.zeros((count,), jnp.int32).at[block_slot].set(jnp.arange(count, dtype=jnp.int32))
    state = rhs.reshape(count, B, NRHS)
    solved = []
    for column in range(2):
        stored = block_slot[column].astype(jnp.int32)
        tile = lax.dynamic_slice_in_dim(panel, stored * B, B, 0)[:, column * B:(column + 1) * B]
        block_state = lax.dynamic_index_in_dim(state, stored, 0, keepdims=False)
        result = lax.linalg.triangular_solve(jnp.tril(tile.astype(jnp.float32)), block_state, left_side=True, lower=True)
        result = result.astype(jnp.bfloat16)
        solved.append(result)
        term = jnp.dot(panel[:, column * B:(column + 1) * B].astype(jnp.float32), result.astype(jnp.float32), preferred_element_type=jnp.float32)
        term = term.reshape(count, B, NRHS)
        state = state - jnp.where((order > column)[:, None, None], term, 0.0)
    first = solved[0].astype(jnp.float32)[None]
    second = solved[1].astype(jnp.float32)[None]
    final = jnp.where((order == 0)[:, None, None], first, jnp.where((order == 1)[:, None, None], second, state))
    mean_part = jnp.dot(target[0], solved[0].astype(jnp.float32), precision=lax.Precision.HIGHEST)
    mean_part = mean_part + jnp.dot(target[1], solved[1].astype(jnp.float32), precision=lax.Precision.HIGHEST)
    return (final.reshape(count * B, NRHS), mean_part)
```

```python
import functools

import jax
import jax.numpy as jnp
from jax import lax
from jax.experimental import pallas as pl
from jax.experimental.pallas import tpu as pltpu
from jax.sharding import PartitionSpec as P

B = 1024
W = 256
NY, NZ, NC = 4, 8, 8
CH = 256
NCH = B // CH
BASE = 16
F32, BF16 = jnp.float32, jnp.bfloat16
MESH = pl.DeviceIdType.MESH


def dot(a, b):
    return jnp.dot(a, b, preferred_element_type=F32)


def split(x):
    hi = x.astype(BF16)
    return hi, (x - hi.astype(F32)).astype(BF16)


def iota(shape, dim):
    return lax.broadcasted_iota(jnp.int32, shape, dim)


def spread_matrix():
    shape = (128, BASE * 128)
    lane = iota(shape, 1)
    return jnp.where(iota(shape, 0) == (lane % 128) // BASE * BASE + lane // 128, 1.0, 0.0).astype(BF16)


def invert_small(blocks, spread):
    groups = len(blocks)
    lane = iota((BASE, 128), 1)
    packed = []
    for block in blocks:
        wide = block.astype(F32)
        acc = jnp.zeros((BASE, 128), F32)
        for b in range(128 // BASE):
            acc = jnp.where(lane // BASE == b, wide[BASE * b : BASE * (b + 1)], acc)
        packed.append(acc)
    packed = jnp.concatenate(packed, axis=0).astype(BF16)
    factors = dot(packed, spread)
    part = [factors[:, 128 * j : 128 * (j + 1)].reshape(groups, BASE, 128) for j in range(BASE)]
    row = iota((groups, BASE, 128), 1)
    diag = part[0]
    for j in range(1, BASE):
        diag = jnp.where(row == j, part[j], diag)
    scale = 1.0 / diag
    x = jnp.where(iota((groups, BASE, 128), 2) % BASE == row, scale, 0.0)
    for j in range(BASE - 1):
        factor = jnp.where(row > j, part[j] * scale, 0.0)
        x = x - factor * x[:, j : j + 1, :]
    return [x[g] for g in range(groups)]


def join_inverses(diag_block):
    groups = B // 128
    spread = spread_matrix()
    blocks = [diag_block(g) for g in range(groups)]
    small = invert_small(blocks, spread)
    r, c = iota((128, 128), 0), iota((128, 128), 1)
    inverses = []
    for g in range(groups):
        tiled = jnp.concatenate([small[g]] * (128 // BASE), axis=0)
        inverses.append(jnp.where(r // BASE == c // BASE, tiled, 0.0))
    size = BASE
    while size < 128:
        mask = ((r // size) % 2 == 1) & (c // size == r // size - 1)
        for g in range(groups):
            off = jnp.where(mask, blocks[g], jnp.zeros_like(blocks[g]))
            hi, lo = split(inverses[g])
            t = dot(jnp.concatenate([off, off], axis=1), jnp.concatenate([hi, lo], axis=0))
            thi, tlo = split(t)
            u = dot(jnp.concatenate([hi, lo], axis=1), jnp.concatenate([thi, thi], axis=0)) + dot(hi, tlo)
            inverses[g] = inverses[g] - u
        size *= 2
    return inverses


def whole_inverse(inverses, corner, b):
    first, second = inverses[2 * b], inverses[2 * b + 1]
    hi, lo = split(first)
    t = dot(jnp.concatenate([corner, corner], axis=1), jnp.concatenate([hi, lo], axis=0))
    thi, tlo = split(t)
    hi2, lo2 = split(second)
    u = dot(jnp.concatenate([hi2, lo2], axis=1), jnp.concatenate([thi, thi], axis=0)) + dot(hi2, tlo)
    full = jnp.concatenate(
        [
            jnp.concatenate([first, jnp.zeros((128, 128), F32)], axis=1),
            jnp.concatenate([-u, second], axis=1),
        ],
        axis=0,
    )
    return split(full)


def kernel(
    slot_ref, target_ref, panel_hbm, rhs_hbm,
    out_hbm, mean_ref,
    panel_0, panel_1, state, diag_0, diag_1, work, inv_hi, inv_lo, solved, x_send, y_recv, z_send, z_recv, gathered, tgt,
    load_sem, store_sem, send_sem, recv_sem, tgt_send, tgt_recv,
):
    row, col = lax.axis_index("row"), lax.axis_index("col")
    y, z = row // NZ, row % NZ
    y_peers = [(lax.rem(y + d, NY) * NZ + z, col) for d in range(1, NY)]
    z_peers = [(y * NZ + lax.rem(z + d, NZ), col) for d in range(1, NZ)]
    c_peers = [(row, lax.rem(col + d, NC)) for d in range(1, NC)]
    tgt[...] = jnp.zeros_like(tgt)
    tgt[col, 0:2, :] = target_ref[...]
    barrier = pltpu.get_barrier_semaphore()
    for peer in y_peers + z_peers + c_peers:
        pl.semaphore_signal(barrier, inc=1, device_id=peer, device_id_type=MESH)

    def load(src, dst, k):
        copy = pltpu.make_async_copy(src, dst, load_sem.at[k])
        copy.start()
        return copy

    blocks = 4
    panel, diag = [panel_0, panel_1], [diag_0, diag_1]

    def load_diag(k, sem):
        for t in range(blocks):
            for b in range(NCH):
                load(
                    panel_hbm.at[pl.ds(t * B + b * CH, CH), pl.ds(k * B + b * CH, CH)],
                    diag[k].at[t, pl.ds(b * CH, CH)],
                    sem,
                )

    def load_column(k, sem):
        for t in range(blocks):
            load(panel_hbm.at[pl.ds(t * B, B), pl.ds(k * B, B)], panel[k].at[t], sem)

    load_diag(0, 0)
    for t in range(blocks):
        load(rhs_hbm.at[pl.ds(t * B, B)], state.at[t], 1)
    load_column(0, 2)
    load_diag(1, 3)
    load_column(1, 4)

    mine = [slot_ref[0] // blocks == row, slot_ref[1] // blocks == row]
    local = [slot_ref[0] % blocks, slot_ref[1] % blocks]

    def wait_load(ref, k):
        pltpu.make_async_copy(ref, ref, load_sem.at[k]).wait()

    def invert(k):
        found = join_inverses(
            lambda g: diag[k][local[k], pl.ds(128 * g, 128), pl.ds(128 * (g % 2), 128)]
        )
        for b in range(NCH):
            corner = diag[k][local[k], pl.ds(256 * b + 128, 128), pl.ds(0, 128)]
            inv_hi[b], inv_lo[b] = whole_inverse(found, corner, b)

    def send(src, dst, k, c, stage, peer):
        pltpu.make_async_remote_copy(
            src_ref=src, dst_ref=dst, send_sem=send_sem.at[k, c, stage], recv_sem=recv_sem.at[k, c, stage],
            device_id=peer, device_id_type=MESH,
        ).start()

    def solve(k):
        his, los = [], []
        for b in range(NCH):
            part = work[pl.ds(b * CH, CH), :]
            for a in range(b):
                tile = panel[k][local[k], pl.ds(b * CH, CH), pl.ds(a * CH, CH)]
                part = part - (dot(tile, his[a]) + dot(tile, los[a]))
            hi, lo = split(part)
            ihi, ilo = inv_hi[b], inv_lo[b]
            x = dot(ihi, hi) + (dot(ihi, lo) + dot(ilo, hi))
            hi, lo = split(x)
            his.append(hi)
            los.append(lo)
            masked = jnp.where(mine[k], x, 0.0).astype(BF16)
            for j in range(NY):
                for i in range(NZ):
                    r = 64 * j + 16 * (i // 2)
                    x_send[k, b, j, i] = masked[r : r + 16, 128 * (i % 2) : 128 * (i % 2 + 1)]
            if k == 0 and b == 0:
                pl.semaphore_wait(barrier, NY + NZ + NC - 3)
                for peer in c_peers:
                    pltpu.make_async_remote_copy(
                        src_ref=tgt.at[col], dst_ref=tgt.at[col], send_sem=tgt_send, recv_sem=tgt_recv,
                        device_id=peer, device_id_type=MESH,
                    ).start()
            for d in range(1, NY):
                send(x_send.at[k, b, lax.rem(y + d, NY)], y_recv.at[k, b, d], k, b, 0, y_peers[d - 1])

    def arrived(ref, k, c, stage):
        pltpu.make_async_copy(ref, ref, recv_sem.at[k, c, stage]).wait()

    def reduce_y(k, c):
        arrived(y_recv.at[k, c, pl.ds(1, NY - 1)], k, c, 0)
        z_send[k, c] = (x_send[k, c, y] + y_recv[k, c, 1]) + (y_recv[k, c, 2] + y_recv[k, c, 3])
        for d in range(1, NZ):
            send(z_send.at[k, c, lax.rem(z + d, NZ)], z_recv.at[k, c, d], k, c, 1, z_peers[d - 1])

    def reduce_z(k, c):
        arrived(z_recv.at[k, c, pl.ds(1, NZ - 1)], k, c, 1)
        total = z_send[k, c, z]
        for d in range(1, NZ):
            total = total + z_recv[k, c, d]
        gathered[k, c, y, z] = total
        piece = gathered.at[k, c, y, z]
        for d in range(1, NZ):
            send(piece, piece, k, c, 2, z_peers[d - 1])

    def gather_z(k, c):
        arrived(z_recv.at[k, c, pl.ds(1, NZ - 1)], k, c, 2)
        piece = gathered.at[k, c, y]
        for d in range(1, NY):
            send(piece, piece, k, c, 3, y_peers[d - 1])

    def gather_y(k, c):
        arrived(y_recv.at[k, c, pl.ds(1, NY - 1)], k, c, 3)
        for j in range(NY):
            for i in range(NZ):
                r = 64 * j + 16 * (i // 2)
                solved[k, pl.ds(c * CH + r, 16), pl.ds(128 * (i % 2), 128)] = gathered[k, c, j, i]

    wait_load(diag_0, 0)
    invert(0)
    wait_load(state, 1)
    work[...] = state[local[0]]
    wait_load(panel_0, 2)
    solve(0)
    for c in range(NCH):
        reduce_y(0, c)
    wait_load(diag_1, 3)
    invert(1)
    for c in range(NCH):
        reduce_z(0, c)
    for c in range(NCH):
        gather_z(0, c)
    wait_load(panel_1, 4)
    work[...] = state[local[1]]
    for c in range(NCH):
        gather_y(0, c)
        work[...] = work[...] - dot(panel_0[local[1], :, pl.ds(c * CH, CH)], solved[0, pl.ds(c * CH, CH), :])
    solve(1)

    first_here = [slot_ref[0] == row * blocks + t for t in range(blocks)]
    second_here = [slot_ref[1] == row * blocks + t for t in range(blocks)]

    tile_rows = 256

    def apply_first(t, i):
        rows = pl.ds(pl.multiple_of(i * tile_rows, tile_rows), tile_rows)
        term = dot(panel_0[t, rows, :], solved[0])
        state[t, rows, :] = state[t, rows, :] - term

    def apply_second(t, i):
        rows = pl.ds(pl.multiple_of(i * tile_rows, tile_rows), tile_rows)
        term = dot(panel_1[t, rows, :], solved[1])
        value = state[t, rows, :] - term
        value = jnp.where(second_here[t], solved[1, rows, :].astype(F32), value)
        state[t, rows, :] = jnp.where(first_here[t], solved[0, rows, :].astype(F32), value)
        pltpu.make_async_copy(
            state.at[t, rows], out_hbm.at[pl.ds(t * B + pl.multiple_of(i * tile_rows, tile_rows), tile_rows)], store_sem
        ).start()

    for c in range(NCH):
        reduce_y(1, c)
    for t in range(2):
        lax.fori_loop(0, B // tile_rows, lambda i, _: apply_first(t, i), None)
    for c in range(NCH):
        reduce_z(1, c)
    for t in range(2, 4):
        lax.fori_loop(0, B // tile_rows, lambda i, _: apply_first(t, i), None)
    for c in range(NCH):
        gather_z(1, c)
    pltpu.make_async_copy(tgt.at[pl.ds(0, NC - 1)], tgt.at[pl.ds(0, NC - 1)], tgt_recv).wait()
    for c in range(NCH):
        gather_y(1, c)
    for t in range(blocks):
        lax.fori_loop(0, B // tile_rows, lambda i, _: apply_second(t, i), None)

    mean = jnp.zeros((8, W), F32)
    for d in range(NC):
        rest = tgt[d]
        for _ in range(3):
            piece = rest.astype(BF16)
            rest = rest - piece.astype(F32)
            wide = jnp.concatenate([piece, jnp.zeros_like(piece)], axis=0)
            for k in range(2):
                found = dot(wide, solved[k, pl.ds(128 * d, 128), :])
                mean = mean + jnp.where(iota((8, W), 0) == k, found[0:8], 0.0)
    mean_ref[...] = mean[0:1] + mean[1:2]

    for k in range(2):
        for c in range(NCH):
            for stage, ref in enumerate((y_recv, z_recv, z_recv, y_recv)):
                count = (NY if stage in (0, 3) else NZ) - 1
                sent = ref.at[k, c, pl.ds(1, count)]
                pltpu.make_async_copy(sent, sent, send_sem.at[k, c, stage]).wait()
    pltpu.make_async_copy(tgt.at[pl.ds(0, NC - 1)], tgt.at[pl.ds(0, NC - 1)], tgt_send).wait()
    pltpu.make_async_copy(state, state, store_sem).wait()


def per_device(panel, rhs, block_slot, target):
    rows, width = rhs.shape
    piece = (NY, NZ, 16, 128)
    out, mean = pl.pallas_call(
        kernel,
        out_shape=(jax.ShapeDtypeStruct((rows, width), F32), jax.ShapeDtypeStruct((1, width), F32)),
        in_specs=[
            pl.BlockSpec(memory_space=pltpu.SMEM),
            pl.BlockSpec(memory_space=pltpu.VMEM),
            pl.BlockSpec(memory_space=pl.ANY),
            pl.BlockSpec(memory_space=pl.ANY),
        ],
        out_specs=(pl.BlockSpec(memory_space=pl.ANY), pl.BlockSpec(memory_space=pltpu.VMEM)),
        scratch_shapes=[
            pltpu.VMEM((4, B, B), BF16),
            pltpu.VMEM((4, B, B), BF16),
            pltpu.VMEM((4, B, W), F32),
            pltpu.VMEM((4, B, CH), BF16),
            pltpu.VMEM((4, B, CH), BF16),
            pltpu.VMEM((B, W), F32),
            pltpu.VMEM((NCH, CH, CH), BF16),
            pltpu.VMEM((NCH, CH, CH), BF16),
            pltpu.VMEM((2, B, W), BF16),
            pltpu.VMEM((2, NCH) + piece, BF16),
            pltpu.VMEM((2, NCH) + piece, BF16),
            pltpu.VMEM((2, NCH) + piece[1:], BF16),
            pltpu.VMEM((2, NCH) + piece[1:], BF16),
            pltpu.VMEM((2, NCH) + piece, BF16),
            pltpu.VMEM((NC, 8, 128), F32),
            pltpu.SemaphoreType.DMA((5,)),
            pltpu.SemaphoreType.DMA,
            pltpu.SemaphoreType.DMA((2, NCH, 4)),
            pltpu.SemaphoreType.DMA((2, NCH, 4)),
            pltpu.SemaphoreType.DMA,
            pltpu.SemaphoreType.DMA,
        ],
        compiler_params=pltpu.CompilerParams(
            collective_id=0, has_side_effects=True, vmem_limit_bytes=56 * 2**20
        ),
        name="substitute",
    )(block_slot, target, panel, rhs)
    return out, mean.reshape(width)


def solution(mesh):
    return jax.shard_map(
        per_device,
        mesh=mesh,
        in_specs=(P("row", None), P("row", "col"), P(), P(None, "col")),
        out_specs=(P("row", "col"), P("col")),
        check_vma=False,
    )
```

```python
import functools

import jax
import jax.numpy as jnp
from jax import lax
from jax.experimental import pallas as pl
from jax.experimental.pallas import tpu as pltpu
from jax.sharding import PartitionSpec as P

B = 1024
W = 256
NY, NZ, NC = 4, 8, 8
CH = 256
NCH = B // CH
BASE = 16
F32, BF16 = jnp.float32, jnp.bfloat16
MESH = pl.DeviceIdType.MESH


def dot(a, b):
    return jnp.dot(a, b, preferred_element_type=F32)


def split(x):
    hi = x.astype(BF16)
    return hi, (x - hi.astype(F32)).astype(BF16)


def iota(shape, dim):
    return lax.broadcasted_iota(jnp.int32, shape, dim)


def spread_matrix():
    shape = (128, BASE * 128)
    lane = iota(shape, 1)
    return jnp.where(iota(shape, 0) == (lane % 128) // BASE * BASE + lane // 128, 1.0, 0.0).astype(BF16)


def invert_small(blocks, spread):
    groups = len(blocks)
    lane = iota((BASE, 128), 1)
    packed = []
    for block in blocks:
        wide = block.astype(F32)
        acc = jnp.zeros((BASE, 128), F32)
        for b in range(128 // BASE):
            acc = jnp.where(lane // BASE == b, wide[BASE * b : BASE * (b + 1)], acc)
        packed.append(acc)
    packed = jnp.concatenate(packed, axis=0).astype(BF16)
    factors = dot(packed, spread)
    part = [factors[:, 128 * j : 128 * (j + 1)].reshape(groups, BASE, 128) for j in range(BASE)]
    row = iota((groups, BASE, 128), 1)
    diag = part[0]
    for j in range(1, BASE):
        diag = jnp.where(row == j, part[j], diag)
    scale = 1.0 / diag
    x = jnp.where(iota((groups, BASE, 128), 2) % BASE == row, scale, 0.0)
    for j in range(BASE - 1):
        factor = jnp.where(row > j, part[j] * scale, 0.0)
        x = x - factor * x[:, j : j + 1, :]
    return [x[g] for g in range(groups)]


def join_inverses(diag_block):
    groups = B // 128
    spread = spread_matrix()
    blocks = [diag_block(g) for g in range(groups)]
    small = invert_small(blocks, spread)
    r, c = iota((128, 128), 0), iota((128, 128), 1)
    inverses = []
    for g in range(groups):
        tiled = jnp.concatenate([small[g]] * (128 // BASE), axis=0)
        inverses.append(jnp.where(r // BASE == c // BASE, tiled, 0.0))
    size = BASE
    while size < 128:
        odd = [slice(i, i + size) for i in range(size, 128, 2 * size)]
        mask = (c // size == r // size - 1) & ((r // size) % 2 == 1)
        off = [rows_of(jnp.where(mask, block, jnp.zeros_like(block)), odd) for block in blocks]
        inverses = joined(inverses, off, odd)
        size *= 2
    return inverses


def rows_of(x, parts):
    return jnp.concatenate([x[p] for p in parts], axis=0)


def joined(inverses, off, odd):
    size = odd[0].stop - odd[0].start
    parts = [split(x) for x in inverses]
    low = [(rows_of(hi, odd), rows_of(lo, odd)) for hi, lo in parts]
    t = [split(dot(jnp.concatenate([e, e], axis=1), jnp.concatenate(p, axis=0))) for e, p in zip(off, parts)]

    def spread_rows(x):
        gap = jnp.zeros((size, x.shape[1]), x.dtype)
        return jnp.concatenate([v for i in range(len(odd)) for v in (gap, x[size * i : size * (i + 1)])], axis=0)

    t = [(spread_rows(hi), spread_rows(lo)) for hi, lo in t]
    u = [
        dot(jnp.concatenate([p[0], p[1]], axis=1), jnp.concatenate([q[0], q[0]], axis=0)) for p, q in zip(low, t)
    ]
    v = [dot(p[0], q[1]) for p, q in zip(low, t)]
    out = []
    for x, y, w in zip(inverses, u, v):
        y = y + w
        pieces = []
        for i, p in enumerate(odd):
            pieces += [x[p.start - size : p.start], x[p] - y[size * i : size * (i + 1)]]
        out.append(jnp.concatenate(pieces, axis=0))
    return out


def whole_inverses(inverses, corners):
    parts = [split(x) for x in inverses]
    t = [
        split(dot(jnp.concatenate([e, e], axis=1), jnp.concatenate(parts[2 * b], axis=0)))
        for b, e in enumerate(corners)
    ]
    u = [
        dot(jnp.concatenate(parts[2 * b + 1], axis=1), jnp.concatenate([q[0], q[0]], axis=0)) for b, q in enumerate(t)
    ]
    v = [dot(parts[2 * b + 1][0], q[1]) for b, q in enumerate(t)]
    gap = jnp.zeros((128, 128), BF16)
    out = []
    for b in range(len(corners)):
        low = split(-(u[b] + v[b]))
        out.append(
            [
                jnp.concatenate(
                    [
                        jnp.concatenate([parts[2 * b][i], gap], axis=1),
                        jnp.concatenate([low[i], parts[2 * b + 1][i]], axis=1),
                    ],
                    axis=0,
                )
                for i in range(2)
            ]
        )
    return out


def kernel(
    slot_ref, target_ref, panel_hbm, rhs_hbm,
    state, mean_ref,
    panel_0, panel_1, low_0, diag_0, diag_1, work, inv_hi, inv_lo, solved, x_send, y_recv, z_send, z_recv, gathered, tgt,
    load_sem, send_sem, recv_sem, tgt_send, tgt_recv,
):
    row, col = lax.axis_index("row"), lax.axis_index("col")
    y, z = row // NZ, row % NZ
    y_peers = [(lax.rem(y + d, NY) * NZ + z, col) for d in range(1, NY)]
    z_peers = [(y * NZ + lax.rem(z + d, NZ), col) for d in range(1, NZ)]
    c_peers = [(row, lax.rem(col + d, NC)) for d in range(1, NC)]
    tgt[...] = jnp.zeros_like(tgt)
    tgt[col, 0:2, :] = target_ref[...]
    barrier = pltpu.get_barrier_semaphore()
    for peer in y_peers + z_peers + c_peers:
        pl.semaphore_signal(barrier, inc=1, device_id=peer, device_id_type=MESH)

    def load(src, dst, k):
        copy = pltpu.make_async_copy(src, dst, load_sem.at[k])
        copy.start()
        return copy

    blocks = 4
    panel, diag = [panel_0, panel_1], [diag_0, diag_1]

    def load_diag(k, sem):
        for t in range(blocks):
            for b in range(NCH):
                load(
                    panel_hbm.at[pl.ds(t * B + b * CH, CH), pl.ds(k * B + b * CH, CH)],
                    diag[k].at[t, pl.ds(b * CH, CH)],
                    sem,
                )

    def load_column(k, sem):
        for t in range(blocks):
            load(panel_hbm.at[pl.ds(t * B, B), pl.ds(k * B, B)], panel[k].at[t], sem)

    lower = [(b, a) for b in range(NCH) for a in range(b)]
    load_diag(0, 0)
    for t in range(blocks):
        load(rhs_hbm.at[pl.ds(t * B, B)], state.at[t], 1)
    for t in range(blocks):
        for i, (b, a) in enumerate(lower):
            load(panel_hbm.at[pl.ds(t * B + b * CH, CH), pl.ds(a * CH, CH)], low_0.at[t, i], 5)

    mine = [slot_ref[0] // blocks == row, slot_ref[1] // blocks == row]
    local = [slot_ref[0] % blocks, slot_ref[1] % blocks]

    def wait_load(ref, k):
        pltpu.make_async_copy(ref, ref, load_sem.at[k]).wait()

    def invert(k):
        found = join_inverses(
            lambda g: diag[k][local[k], pl.ds(128 * g, 128), pl.ds(128 * (g % 2), 128)]
        )
        corners = [diag[k][local[k], pl.ds(CH * b + 128, 128), pl.ds(0, 128)] for b in range(NCH)]
        for b, (hi, lo) in enumerate(whole_inverses(found, corners)):
            inv_hi[b], inv_lo[b] = hi, lo

    def send(src, dst, k, c, stage, peer):
        pltpu.make_async_remote_copy(
            src_ref=src, dst_ref=dst, send_sem=send_sem.at[k, c, stage], recv_sem=recv_sem.at[k, c, stage],
            device_id=peer, device_id_type=MESH,
        ).start()

    def solve(k):
        his, los = [], []
        for b in range(NCH):
            part = work[pl.ds(b * CH, CH), :]
            for a in range(b):
                if k == 0:
                    tile = low_0[local[0], lower.index((b, a))]
                else:
                    tile = panel_1[local[1], pl.ds(b * CH, CH), pl.ds(a * CH, CH)]
                part = part - (dot(tile, his[a]) + dot(tile, los[a]))
            hi, lo = split(part)
            ihi, ilo = inv_hi[b], inv_lo[b]
            x = dot(ihi, hi) + (dot(ihi, lo) + dot(ilo, hi))
            hi, lo = split(x)
            his.append(hi)
            los.append(lo)
            masked = jnp.where(mine[k], x, 0.0).astype(BF16)
            for j in range(NY):
                for i in range(NZ):
                    r = 64 * j + 16 * (i // 2)
                    x_send[k, b, j, i] = masked[r : r + 16, 128 * (i % 2) : 128 * (i % 2 + 1)]
            if k == 0 and b == 0:
                pl.semaphore_wait(barrier, NY + NZ + NC - 3)
                for peer in c_peers:
                    pltpu.make_async_remote_copy(
                        src_ref=tgt.at[col], dst_ref=tgt.at[col], send_sem=tgt_send, recv_sem=tgt_recv,
                        device_id=peer, device_id_type=MESH,
                    ).start()
            for d in range(1, NY):
                send(x_send.at[k, b, lax.rem(y + d, NY)], y_recv.at[k, b, d], k, b, 0, y_peers[d - 1])

    def arrived(ref, k, c, stage):
        pltpu.make_async_copy(ref, ref, recv_sem.at[k, c, stage]).wait()

    def reduce_y(k, c):
        arrived(y_recv.at[k, c, pl.ds(1, NY - 1)], k, c, 0)
        z_send[k, c] = (x_send[k, c, y] + y_recv[k, c, 1]) + (y_recv[k, c, 2] + y_recv[k, c, 3])
        for d in range(1, NZ):
            send(z_send.at[k, c, lax.rem(z + d, NZ)], z_recv.at[k, c, d], k, c, 1, z_peers[d - 1])

    def reduce_z(k, c):
        arrived(z_recv.at[k, c, pl.ds(1, NZ - 1)], k, c, 1)
        total = z_send[k, c, z]
        for d in range(1, NZ):
            total = total + z_recv[k, c, d]
        gathered[k, c, y, z] = total
        piece = gathered.at[k, c, y, z]
        for d in range(1, NZ):
            send(piece, piece, k, c, 2, z_peers[d - 1])

    def gather_z(k, c):
        arrived(z_recv.at[k, c, pl.ds(1, NZ - 1)], k, c, 2)
        piece = gathered.at[k, c, y]
        for d in range(1, NY):
            send(piece, piece, k, c, 3, y_peers[d - 1])

    def gather_y(k, c):
        arrived(y_recv.at[k, c, pl.ds(1, NY - 1)], k, c, 3)
        for j in range(NY):
            for i in range(NZ):
                r = 64 * j + 16 * (i // 2)
                solved[k, pl.ds(c * CH + r, 16), pl.ds(128 * (i % 2), 128)] = gathered[k, c, j, i]

    wait_load(diag_0, 0)
    load_diag(1, 3)
    load_column(0, 2)
    load_column(1, 4)
    invert(0)
    wait_load(state, 1)
    work[...] = state[local[0]]
    wait_load(low_0, 5)
    solve(0)
    for c in range(NCH):
        reduce_y(0, c)
    wait_load(diag_1, 3)
    invert(1)
    for c in range(NCH):
        reduce_z(0, c)
    work[...] = state[local[1]]
    for c in range(NCH):
        gather_z(0, c)
    wait_load(panel_0, 2)
    wait_load(panel_1, 4)
    for c in range(NCH):
        gather_y(0, c)
        work[...] = work[...] - dot(panel_0[local[1], :, pl.ds(c * CH, CH)], solved[0, pl.ds(c * CH, CH), :])
    solve(1)

    def apply_first(t):
        state[t] = state[t] - dot(panel_0[t], solved[0])

    def apply_second(t, c):
        part = pl.ds(c * CH, CH)
        value = state[t] - dot(panel_1[t, :, part], solved[1, part, :])
        if c == NCH - 1:
            value = jnp.where(slot_ref[1] == row * blocks + t, solved[1].astype(F32), value)
            value = jnp.where(slot_ref[0] == row * blocks + t, solved[0].astype(F32), value)
        state[t] = value

    def mean_terms(k):
        mean = jnp.zeros((8, W), F32)
        for d in range(NC):
            rest = tgt[d]
            for _ in range(3):
                piece = rest.astype(BF16)
                rest = rest - piece.astype(F32)
                wide = jnp.concatenate([piece, jnp.zeros_like(piece)], axis=0)
                mean = mean + dot(wide, solved[k, pl.ds(128 * d, 128), :])[0:8]
        return mean[k : k + 1]

    for c in range(NCH):
        reduce_y(1, c)
    apply_first(0)
    apply_first(1)
    for c in range(NCH):
        reduce_z(1, c)
    apply_first(2)
    apply_first(3)
    for c in range(NCH):
        gather_z(1, c)
    pltpu.make_async_copy(tgt.at[pl.ds(0, NC - 1)], tgt.at[pl.ds(0, NC - 1)], tgt_recv).wait()
    mean = mean_terms(0)
    for c in range(NCH):
        gather_y(1, c)
        for t in range(blocks):
            apply_second(t, c)
    mean_ref[...] = (mean + mean_terms(1)).reshape(W)

    for k in range(2):
        for c in range(NCH):
            for stage, ref in enumerate((y_recv, z_recv, z_recv, y_recv)):
                count = (NY if stage in (0, 3) else NZ) - 1
                sent = ref.at[k, c, pl.ds(1, count)]
                pltpu.make_async_copy(sent, sent, send_sem.at[k, c, stage]).wait()
    pltpu.make_async_copy(tgt.at[pl.ds(0, NC - 1)], tgt.at[pl.ds(0, NC - 1)], tgt_send).wait()


def per_device(panel, rhs, block_slot, target):
    rows, width = rhs.shape
    piece = (NY, NZ, 16, 128)
    out, mean = pl.pallas_call(
        kernel,
        out_shape=(pltpu.VMEM((rows // B, B, width), F32), jax.ShapeDtypeStruct((width,), F32)),
        in_specs=[
            pl.BlockSpec(memory_space=pltpu.SMEM),
            pl.BlockSpec(memory_space=pltpu.VMEM),
            pl.BlockSpec(memory_space=pl.ANY),
            pl.BlockSpec(memory_space=pl.ANY),
        ],
        out_specs=(pl.BlockSpec(memory_space=pltpu.VMEM), pl.BlockSpec(memory_space=pltpu.VMEM)),
        scratch_shapes=[
            pltpu.VMEM((4, B, B), BF16),
            pltpu.VMEM((4, B, B), BF16),
            pltpu.VMEM((4, 6, CH, CH), BF16),
            pltpu.VMEM((4, B, CH), BF16),
            pltpu.VMEM((4, B, CH), BF16),
            pltpu.VMEM((B, W), F32),
            pltpu.VMEM((NCH, CH, CH), BF16),
            pltpu.VMEM((NCH, CH, CH), BF16),
            pltpu.VMEM((2, B, W), BF16),
            pltpu.VMEM((2, NCH) + piece, BF16),
            pltpu.VMEM((2, NCH) + piece, BF16),
            pltpu.VMEM((2, NCH) + piece[1:], BF16),
            pltpu.VMEM((2, NCH) + piece[1:], BF16),
            pltpu.VMEM((2, NCH) + piece, BF16),
            pltpu.VMEM((NC, 8, 128), F32),
            pltpu.SemaphoreType.DMA((6,)),
            pltpu.SemaphoreType.DMA((2, NCH, 4)),
            pltpu.SemaphoreType.DMA((2, NCH, 4)),
            pltpu.SemaphoreType.DMA,
            pltpu.SemaphoreType.DMA,
        ],
        compiler_params=pltpu.CompilerParams(
            collective_id=0, has_side_effects=True, vmem_limit_bytes=56 * 2**20
        ),
        name="substitute",
    )(block_slot, target, panel, rhs)
    return out.reshape(rows, width), mean


def solution(mesh):
    return jax.shard_map(
        per_device,
        mesh=mesh,
        in_specs=(P("row", None), P("row", "col"), P(), P(None, "col")),
        out_specs=(P("row", "col"), P("col")),
        check_vma=False,
    )
```

```python
import functools

import jax
import jax.numpy as jnp
from jax import lax
from jax.experimental import pallas as pl
from jax.experimental.pallas import tpu as pltpu
from jax.sharding import PartitionSpec as P

B = 1024
W = 256
NY, NZ, NC = 4, 8, 8
CH = 256
NCH = B // CH
BASE = 16
PIECE = CH // 8
F32, BF16 = jnp.float32, jnp.bfloat16
MESH = pl.DeviceIdType.MESH


def dot(a, b):
    return jnp.dot(a, b, preferred_element_type=F32)


def split(x):
    hi = x.astype(BF16)
    return hi, (x - hi.astype(F32)).astype(BF16)


def iota(shape, dim):
    return lax.broadcasted_iota(jnp.int32, shape, dim)


def spread_matrix():
    shape = (128, BASE * 128)
    lane = iota(shape, 1)
    return jnp.where(iota(shape, 0) == (lane % 128) // BASE * BASE + lane // 128, 1.0, 0.0).astype(BF16)


def invert_small(blocks, spread):
    groups = len(blocks)
    lane = iota((BASE, 128), 1)
    packed = []
    for block in blocks:
        wide = block.astype(F32)
        acc = jnp.zeros((BASE, 128), F32)
        for b in range(128 // BASE):
            acc = jnp.where(lane // BASE == b, wide[BASE * b : BASE * (b + 1)], acc)
        packed.append(acc)
    packed = jnp.concatenate(packed, axis=0).astype(BF16)
    factors = dot(packed, spread)
    part = [factors[:, 128 * j : 128 * (j + 1)].reshape(groups, BASE, 128) for j in range(BASE)]
    row = iota((groups, BASE, 128), 1)
    diag = part[0]
    for j in range(1, BASE):
        diag = jnp.where(row == j, part[j], diag)
    scale = 1.0 / diag
    x = jnp.where(iota((groups, BASE, 128), 2) % BASE == row, scale, 0.0)
    for j in range(BASE - 1):
        factor = jnp.where(row > j, part[j] * scale, 0.0)
        x = x - factor * x[:, j : j + 1, :]
    return [x[g] for g in range(groups)]


def join_inverses(diag_block):
    groups = B // 128
    spread = spread_matrix()
    blocks = [diag_block(g) for g in range(groups)]
    small = invert_small(blocks, spread)
    r, c = iota((128, 128), 0), iota((128, 128), 1)
    inverses = []
    for g in range(groups):
        tiled = jnp.concatenate([small[g]] * (128 // BASE), axis=0)
        inverses.append(jnp.where(r // BASE == c // BASE, tiled, 0.0))
    size = BASE
    while size < 128:
        odd = [slice(i, i + size) for i in range(size, 128, 2 * size)]
        mask = (c // size == r // size - 1) & ((r // size) % 2 == 1)
        off = [rows_of(jnp.where(mask, block, jnp.zeros_like(block)), odd) for block in blocks]
        inverses = joined(inverses, off, odd)
        size *= 2
    return inverses


def rows_of(x, parts):
    return jnp.concatenate([x[p] for p in parts], axis=0)


def joined(inverses, off, odd):
    size = odd[0].stop - odd[0].start
    parts = [split(x) for x in inverses]
    low = [(rows_of(hi, odd), rows_of(lo, odd)) for hi, lo in parts]
    t = [split(dot(jnp.concatenate([e, e], axis=1), jnp.concatenate(p, axis=0))) for e, p in zip(off, parts)]

    def spread_rows(x):
        gap = jnp.zeros((size, x.shape[1]), x.dtype)
        return jnp.concatenate([v for i in range(len(odd)) for v in (gap, x[size * i : size * (i + 1)])], axis=0)

    t = [(spread_rows(hi), spread_rows(lo)) for hi, lo in t]
    u = [
        dot(jnp.concatenate([p[0], p[1]], axis=1), jnp.concatenate([q[0], q[0]], axis=0)) for p, q in zip(low, t)
    ]
    v = [dot(p[0], q[1]) for p, q in zip(low, t)]
    out = []
    for x, y, w in zip(inverses, u, v):
        y = y + w
        pieces = []
        for i, p in enumerate(odd):
            pieces += [x[p.start - size : p.start], x[p] - y[size * i : size * (i + 1)]]
        out.append(jnp.concatenate(pieces, axis=0))
    return out


def whole_inverses(inverses, corners):
    parts = [split(x) for x in inverses]
    t = [
        split(dot(jnp.concatenate([e, e], axis=1), jnp.concatenate(parts[2 * b], axis=0)))
        for b, e in enumerate(corners)
    ]
    u = [
        dot(jnp.concatenate(parts[2 * b + 1], axis=1), jnp.concatenate([q[0], q[0]], axis=0)) for b, q in enumerate(t)
    ]
    v = [dot(parts[2 * b + 1][0], q[1]) for b, q in enumerate(t)]
    gap = jnp.zeros((128, 128), BF16)
    out = []
    for b in range(len(corners)):
        low = split(-(u[b] + v[b]))
        out.append(
            [
                jnp.concatenate(
                    [
                        jnp.concatenate([parts[2 * b][i], gap], axis=1),
                        jnp.concatenate([low[i], parts[2 * b + 1][i]], axis=1),
                    ],
                    axis=0,
                )
                for i in range(2)
            ]
        )
    return out


def kernel(
    slot_ref, target_ref, panel_hbm, rhs_hbm,
    state, mean_ref,
    panel_0, panel_1, low_0, diag_0, diag_1, work, inv_hi, inv_lo, solved, x_send, near_recv, z_send, z_recv, tgt,
    load_sem, send_sem, recv_sem, tgt_send, tgt_recv,
):
    row, col = lax.axis_index("row"), lax.axis_index("col")
    y, z = row // NZ, row % NZ

    def half(c):
        return lax.rem(z + c % 2, 2)

    def near(c, dy, flip):
        step = flip * (1 - 2 * half(c))
        return (lax.rem(y + dy, NY) * NZ + lax.rem(z + step + NZ, NZ), col)

    def near_rows(c, dy, flip):
        slot = lax.rem(y + dy, NY) * 2 + half(c) + flip * (1 - 2 * half(c))
        return pl.ds(pl.multiple_of(c * CH + slot * PIECE, PIECE), PIECE)

    around = [(2, 1), (1, 1), (3, 1), (2, 0), (1, 0), (3, 0), (0, 1)]
    along = [4, 2, 6]
    z_peers = [(y * NZ + lax.rem(z + d, NZ), col) for d in along]
    c_peers = [(row, lax.rem(col + d, NC)) for d in range(1, NC)]
    tgt[...] = jnp.zeros_like(tgt)
    tgt[col, 0:2, :] = target_ref[...]
    barrier = pltpu.get_barrier_semaphore()
    near_peers = [near(0, dy, flip) for dy, flip in around] + [near(1, dy, flip) for dy, flip in around if flip]
    peers = near_peers + z_peers + c_peers
    for peer in peers:
        pl.semaphore_signal(barrier, inc=1, device_id=peer, device_id_type=MESH)

    def load(src, dst, k):
        copy = pltpu.make_async_copy(src, dst, load_sem.at[k])
        copy.start()
        return copy

    blocks = 4
    panel, diag = [panel_0, panel_1], [diag_0, diag_1]

    def load_diag(k, sem):
        for t in range(blocks):
            for b in range(NCH):
                load(
                    panel_hbm.at[pl.ds(t * B + b * CH, CH), pl.ds(k * B + b * CH, CH)],
                    diag[k].at[t, pl.ds(b * CH, CH)],
                    sem,
                )

    def load_column(k, sem):
        for t in range(blocks):
            load(panel_hbm.at[pl.ds(t * B, B), pl.ds(k * B, B)], panel[k].at[t], sem)

    lower = [(b, a) for b in range(NCH) for a in range(b)]
    load_diag(0, 0)
    for t in range(blocks):
        load(rhs_hbm.at[pl.ds(t * B, B)], state.at[t], 1)
    for t in range(blocks):
        for i, (b, a) in enumerate(lower):
            load(panel_hbm.at[pl.ds(t * B + b * CH, CH), pl.ds(a * CH, CH)], low_0.at[t, i], 5)

    mine = [slot_ref[0] // blocks == row, slot_ref[1] // blocks == row]
    local = [slot_ref[0] % blocks, slot_ref[1] % blocks]

    def wait_load(ref, k):
        pltpu.make_async_copy(ref, ref, load_sem.at[k]).wait()

    def invert(k):
        found = join_inverses(
            lambda g: diag[k][local[k], pl.ds(128 * g, 128), pl.ds(128 * (g % 2), 128)]
        )
        corners = [diag[k][local[k], pl.ds(CH * b + 128, 128), pl.ds(0, 128)] for b in range(NCH)]
        for b, (hi, lo) in enumerate(whole_inverses(found, corners)):
            inv_hi[b], inv_lo[b] = hi, lo

    def send(src, dst, k, c, stage, peer):
        pltpu.make_async_remote_copy(
            src_ref=src, dst_ref=dst, send_sem=send_sem.at[k, c, stage], recv_sem=recv_sem.at[k, c, stage],
            device_id=peer, device_id_type=MESH,
        ).start()

    def solve(k):
        his, los = [], []
        for b in range(NCH):
            part = work[pl.ds(b * CH, CH), :]
            for a in range(b):
                if k == 0:
                    tile = low_0[local[0], lower.index((b, a))]
                else:
                    tile = panel_1[local[1], pl.ds(b * CH, CH), pl.ds(a * CH, CH)]
                part = part - (dot(tile, his[a]) + dot(tile, los[a]))
            hi, lo = split(part)
            ihi, ilo = inv_hi[b], inv_lo[b]
            x = dot(ihi, hi) + (dot(ihi, lo) + dot(ilo, hi))
            hi, lo = split(x)
            his.append(hi)
            los.append(lo)
            masked = jnp.where(mine[k], x, 0.0).astype(BF16)
            x_send[k, pl.ds(b * CH, CH), :] = masked
            if k == 0 and b == 0:
                pl.semaphore_wait(barrier, len(peers))
                for peer in c_peers:
                    pltpu.make_async_remote_copy(
                        src_ref=tgt.at[col], dst_ref=tgt.at[col], send_sem=tgt_send, recv_sem=tgt_recv,
                        device_id=peer, device_id_type=MESH,
                    ).start()
            for dy, flip in around:
                send(x_send.at[k, near_rows(b, dy, flip)], near_recv.at[k, b, dy * 2 + flip], k, b, 0, near(b, dy, flip))

    def arrived(ref, k, c, stage):
        pltpu.make_async_copy(ref, ref, recv_sem.at[k, c, stage]).wait()

    def reduce_near(k, c):
        arrived(near_recv.at[k, c, pl.ds(1, 7)], k, c, 0)
        total = x_send[k, near_rows(c, 0, 0), :]
        for d in range(1, 8):
            total = total + near_recv[k, c, d]
        z_send[k, c] = total
        for d, peer in zip(along, z_peers):
            send(z_send.at[k, c], z_recv.at[k, c, d // 2], k, c, 1, peer)

    def reduce_along(k, c):
        arrived(z_recv.at[k, c, pl.ds(1, 3)], k, c, 1)
        total = (z_send[k, c] + z_recv[k, c, 1]) + (z_recv[k, c, 2] + z_recv[k, c, 3])
        mine_here = near_rows(c, 0, 0)
        solved[k, mine_here, :] = total
        piece = solved.at[k, mine_here]
        for dy, flip in around:
            send(piece, piece, k, c, 2, near(c, dy, flip))

    def gather(k, c):
        arrived(near_recv.at[k, c, pl.ds(1, 7)], k, c, 2)

    wait_load(diag_0, 0)
    load_diag(1, 3)
    load_column(0, 2)
    load_column(1, 4)
    invert(0)
    wait_load(state, 1)
    work[...] = state[local[0]]
    wait_load(low_0, 5)
    solve(0)
    for c in range(NCH):
        reduce_near(0, c)
    wait_load(diag_1, 3)
    invert(1)
    for c in range(NCH):
        reduce_along(0, c)
    work[...] = state[local[1]]
    wait_load(panel_0, 2)
    wait_load(panel_1, 4)
    for c in range(NCH):
        gather(0, c)
        work[...] = work[...] - dot(panel_0[local[1], :, pl.ds(c * CH, CH)], solved[0, pl.ds(c * CH, CH), :])
    solve(1)

    def apply_first(t):
        state[t] = state[t] - dot(panel_0[t], solved[0])

    def apply_second(t, c):
        part = pl.ds(c * CH, CH)
        value = state[t] - dot(panel_1[t, :, part], solved[1, part, :])
        if c == NCH - 1:
            value = jnp.where(slot_ref[1] == row * blocks + t, solved[1].astype(F32), value)
            value = jnp.where(slot_ref[0] == row * blocks + t, solved[0].astype(F32), value)
        state[t] = value

    def mean_weights():
        rest = jnp.concatenate([tgt[d] for d in range(NC)], axis=1)
        parts = []
        for _ in range(3):
            parts.append(rest.astype(BF16).astype(F32))
            rest = rest - parts[-1]
        return jnp.concatenate(parts + [jnp.zeros_like(rest)], axis=0).astype(BF16)

    def mean_terms(weights, k):
        found = dot(weights, solved[k])
        return found[k : k + 1] + found[8 + k : 9 + k] + found[16 + k : 17 + k]

    apply_first(0)
    for c in range(NCH):
        reduce_near(1, c)
    apply_first(1)
    apply_first(2)
    for c in range(NCH):
        reduce_along(1, c)
    apply_first(3)
    pltpu.make_async_copy(tgt.at[pl.ds(0, NC - 1)], tgt.at[pl.ds(0, NC - 1)], tgt_recv).wait()
    weights = mean_weights()
    mean = mean_terms(weights, 0)
    for c in range(NCH):
        gather(1, c)
        for t in range(blocks):
            apply_second(t, c)
    mean_ref[...] = (mean + mean_terms(weights, 1)).reshape(W)

    for k in range(2):
        for c in range(NCH):
            for stage, sent in enumerate((near_recv.at[k, c, pl.ds(1, 7)], z_recv.at[k, c, pl.ds(1, 3)], near_recv.at[k, c, pl.ds(1, 7)])):
                pltpu.make_async_copy(sent, sent, send_sem.at[k, c, stage]).wait()
    pltpu.make_async_copy(tgt.at[pl.ds(0, NC - 1)], tgt.at[pl.ds(0, NC - 1)], tgt_send).wait()


def per_device(panel, rhs, block_slot, target):
    rows, width = rhs.shape
    piece = (PIECE, W)
    out, mean = pl.pallas_call(
        kernel,
        out_shape=(pltpu.VMEM((rows // B, B, width), F32), jax.ShapeDtypeStruct((width,), F32)),
        in_specs=[
            pl.BlockSpec(memory_space=pltpu.SMEM),
            pl.BlockSpec(memory_space=pltpu.VMEM),
            pl.BlockSpec(memory_space=pl.ANY),
            pl.BlockSpec(memory_space=pl.ANY),
        ],
        out_specs=(pl.BlockSpec(memory_space=pltpu.VMEM), pl.BlockSpec(memory_space=pltpu.VMEM)),
        scratch_shapes=[
            pltpu.VMEM((4, B, B), BF16),
            pltpu.VMEM((4, B, B), BF16),
            pltpu.VMEM((4, 6, CH, CH), BF16),
            pltpu.VMEM((4, B, CH), BF16),
            pltpu.VMEM((4, B, CH), BF16),
            pltpu.VMEM((B, W), F32),
            pltpu.VMEM((NCH, CH, CH), BF16),
            pltpu.VMEM((NCH, CH, CH), BF16),
            pltpu.VMEM((2, B, W), BF16),
            pltpu.VMEM((2, B, W), BF16),
            pltpu.VMEM((2, NCH, 8) + piece, BF16),
            pltpu.VMEM((2, NCH) + piece, BF16),
            pltpu.VMEM((2, NCH, 4) + piece, BF16),
            pltpu.VMEM((NC, 8, 128), F32),
            pltpu.SemaphoreType.DMA((6,)),
            pltpu.SemaphoreType.DMA((2, NCH, 3)),
            pltpu.SemaphoreType.DMA((2, NCH, 3)),
            pltpu.SemaphoreType.DMA,
            pltpu.SemaphoreType.DMA,
        ],
        compiler_params=pltpu.CompilerParams(
            collective_id=0, has_side_effects=True, vmem_limit_bytes=56 * 2**20
        ),
        name="substitute",
    )(block_slot, target, panel, rhs)
    return out.reshape(rows, width), mean


def solution(mesh):
    return jax.shard_map(
        per_device,
        mesh=mesh,
        in_specs=(P("row", None), P("row", "col"), P(), P(None, "col")),
        out_specs=(P("row", "col"), P("col")),
        check_vma=False,
    )
```

```python
import functools

import jax
import jax.numpy as jnp
from jax import lax
from jax.experimental import pallas as pl
from jax.experimental.pallas import tpu as pltpu
from jax.sharding import PartitionSpec as P

B = 1024
W = 256
NY, NZ, NC = 4, 8, 8
CH = 256
NCH = B // CH
BASE = 16
PIECE = CH // 8
PARTS = 10
PARTS_M, PARTS_0, PARTS_1 = [0, 1], [2, 3, 4, 5], [6, 7, 8, 9]
F32, BF16 = jnp.float32, jnp.bfloat16
MESH = pl.DeviceIdType.MESH


def dot(a, b):
    return jnp.dot(a, b, preferred_element_type=F32)


def split(x):
    hi = x.astype(BF16)
    return hi, (x - hi.astype(F32)).astype(BF16)


def iota(shape, dim):
    return lax.broadcasted_iota(jnp.int32, shape, dim)


def spread_matrix():
    shape = (128, BASE * 128)
    lane = iota(shape, 1)
    return jnp.where(iota(shape, 0) == (lane % 128) // BASE * BASE + lane // 128, 1.0, 0.0).astype(BF16)


def invert_small(blocks, spread):
    groups = len(blocks)
    lane = iota((BASE, 128), 1)
    packed = []
    for block in blocks:
        wide = block.astype(F32)
        acc = jnp.zeros((BASE, 128), F32)
        for b in range(128 // BASE):
            acc = jnp.where(lane // BASE == b, wide[BASE * b : BASE * (b + 1)], acc)
        packed.append(acc)
    packed = jnp.concatenate(packed, axis=0).astype(BF16)
    factors = dot(packed, spread)
    part = [factors[:, 128 * j : 128 * (j + 1)].reshape(groups, BASE, 128) for j in range(BASE)]
    row = iota((groups, BASE, 128), 1)
    diag = part[0]
    for j in range(1, BASE):
        diag = jnp.where(row == j, part[j], diag)
    scale = 1.0 / diag
    x = jnp.where(iota((groups, BASE, 128), 2) % BASE == row, scale, 0.0)
    for j in range(BASE - 1):
        factor = jnp.where(row > j, part[j] * scale, 0.0)
        x = x - factor * x[:, j : j + 1, :]
    return [x[g] for g in range(groups)]


def join_inverses(diag_block):
    groups = B // 128
    spread = spread_matrix()
    blocks = [diag_block(g) for g in range(groups)]
    small = invert_small(blocks, spread)
    r, c = iota((128, 128), 0), iota((128, 128), 1)
    inverses = []
    for g in range(groups):
        tiled = jnp.concatenate([small[g]] * (128 // BASE), axis=0)
        inverses.append(jnp.where(r // BASE == c // BASE, tiled, 0.0))
    size = BASE
    while size < 128:
        odd = [slice(i, i + size) for i in range(size, 128, 2 * size)]
        mask = (c // size == r // size - 1) & ((r // size) % 2 == 1)
        off = [rows_of(jnp.where(mask, block, jnp.zeros_like(block)), odd) for block in blocks]
        inverses = joined(inverses, off, odd)
        size *= 2
    return inverses


def rows_of(x, parts):
    return jnp.concatenate([x[p] for p in parts], axis=0)


def joined(inverses, off, odd):
    size = odd[0].stop - odd[0].start
    parts = [split(x) for x in inverses]
    low = [(rows_of(hi, odd), rows_of(lo, odd)) for hi, lo in parts]
    t = [split(dot(jnp.concatenate([e, e], axis=1), jnp.concatenate(p, axis=0))) for e, p in zip(off, parts)]

    def spread_rows(x):
        gap = jnp.zeros((size, x.shape[1]), x.dtype)
        return jnp.concatenate([v for i in range(len(odd)) for v in (gap, x[size * i : size * (i + 1)])], axis=0)

    t = [(spread_rows(hi), spread_rows(lo)) for hi, lo in t]
    u = [
        dot(jnp.concatenate([p[0], p[1]], axis=1), jnp.concatenate([q[0], q[0]], axis=0)) for p, q in zip(low, t)
    ]
    v = [dot(p[0], q[1]) for p, q in zip(low, t)]
    out = []
    for x, y, w in zip(inverses, u, v):
        y = y + w
        pieces = []
        for i, p in enumerate(odd):
            pieces += [x[p.start - size : p.start], x[p] - y[size * i : size * (i + 1)]]
        out.append(jnp.concatenate(pieces, axis=0))
    return out


def whole_inverses(inverses, corners):
    parts = [split(x) for x in inverses]
    t = [
        split(dot(jnp.concatenate([e, e], axis=1), jnp.concatenate(parts[2 * b], axis=0)))
        for b, e in enumerate(corners)
    ]
    u = [
        dot(jnp.concatenate(parts[2 * b + 1], axis=1), jnp.concatenate([q[0], q[0]], axis=0)) for b, q in enumerate(t)
    ]
    v = [dot(parts[2 * b + 1][0], q[1]) for b, q in enumerate(t)]
    gap = jnp.zeros((128, 128), BF16)
    out = []
    for b in range(len(corners)):
        low = split(-(u[b] + v[b]))
        out.append(
            [
                jnp.concatenate(
                    [
                        jnp.concatenate([parts[2 * b][i], gap], axis=1),
                        jnp.concatenate([low[i], parts[2 * b + 1][i]], axis=1),
                    ],
                    axis=0,
                )
                for i in range(2)
            ]
        )
    return out


def prepare(
    slot_ref, panel_hbm, rhs_hbm, out, diag, low, right, cross, inv_hi, inv_lo, load_sem,
):
    row, col = lax.axis_index("row"), lax.axis_index("col")
    blocks = 4
    lower = [(b, a) for b in range(NCH) for a in range(b)]

    def load(src, dst, k):
        pltpu.make_async_copy(src, dst, load_sem.at[k]).start()

    def wait_load(ref, k):
        pltpu.make_async_copy(ref, ref, load_sem.at[k]).wait()

    def job(k):
        start = (slot_ref[k] % blocks) * B
        at = lambda b: pl.ds(pl.multiple_of(start + b * CH, CH), CH)
        whole = pl.ds(pl.multiple_of(start, B), B)
        for b in range(NCH):
            load(panel_hbm.at[at(b), pl.ds(k * B + b * CH, CH)], diag.at[pl.ds(b * CH, CH)], 0)
        load(rhs_hbm.at[whole], right, 1)
        if k == 1:
            load(panel_hbm.at[whole, pl.ds(pl.multiple_of(col * 128, 128), 128)], cross, 2)
        for i, (b, a) in enumerate(lower):
            load(panel_hbm.at[at(b), pl.ds(k * B + a * CH, CH)], low.at[i], 3)
        wait_load(diag, 0)
        found = join_inverses(lambda g: diag[pl.ds(128 * g, 128), pl.ds(128 * (g % 2), 128)])
        corners = [diag[pl.ds(CH * b + 128, 128), pl.ds(0, 128)] for b in range(NCH)]
        for b, (hi, lo) in enumerate(whole_inverses(found, corners)):
            inv_hi[b], inv_lo[b] = hi, lo
        wait_load(right, 1)
        if k == 1:
            wait_load(cross, 2)
        wait_load(low, 3)
        his, los = [], []
        for b in range(NCH):
            rows = pl.ds(b * CH, CH)
            part = right[rows, :]
            if k == 1:
                part = jnp.concatenate([part, cross[rows, :].astype(F32)], axis=1)
            for a in range(b):
                tile = low[lower.index((b, a))]
                part = part - (dot(tile, his[a]) + dot(tile, los[a]))
            hi, lo = split(part)
            ihi, ilo = inv_hi[b], inv_lo[b]
            x = dot(ihi, hi) + (dot(ihi, lo) + dot(ilo, hi))
            hi, lo = split(x)
            his.append(hi)
            los.append(lo)
            out[pl.ds((PARTS_0[b] if k == 0 else PARTS_1[b]) * CH, CH), :] = hi[:, :W]
            if k == 1:
                out[pl.ds(PARTS_M[b // 2] * CH, CH), pl.ds(128 * (b % 2), 128)] = hi[:, W:]

    spans = [[(PARTS_0[0], NCH)], [(PARTS_M[0], 2), (PARTS_1[0], NCH)]]
    for k in range(2):
        mine = slot_ref[k] // blocks == row
        pl.when(mine)(functools.partial(job, k))

        @pl.when(jnp.logical_not(mine))
        def _():
            for first, count in spans[k]:
                out[pl.ds(first * CH, count * CH), :] = jnp.zeros((count * CH, W), BF16)


def kernel(
    slot_ref, target_ref, x_send, panel_hbm, rhs_hbm,
    state, mean_ref,
    panel_0, panel_1, second, second_wide,
    near_recv, z_send, z_recv, got, middle, tgt,
    load_sem, send_sem, recv_sem, x_sem, core_sem, pass_sem, tgt_sem,
):
    row, col = lax.axis_index("row"), lax.axis_index("col")
    y, z = row // NZ, row % NZ

    def half(q):
        return lax.rem(z + q % 2, 2)

    def near(q, dy, flip):
        step = flip * (1 - 2 * half(q))
        return (lax.rem(y + dy, NY) * NZ + lax.rem(z + step + NZ, NZ), col)

    def near_rows(q, dy, flip):
        slot = lax.rem(y + dy, NY) * 2 + half(q) + flip * (1 - 2 * half(q))
        return pl.ds(pl.multiple_of(q * CH + slot * PIECE, PIECE), PIECE)

    around = [(2, 1), (1, 1), (3, 1), (2, 0), (1, 0), (3, 0), (0, 1)]
    along = [4, 2, 6]
    z_peers = [(y * NZ + lax.rem(z + d, NZ), col) for d in along]
    c_peers = [(row, lax.rem(col + d, NC)) for d in range(1, NC)]
    x_cols = [lax.rem(col + d, NC) for d in (4, 2, 6)]
    sibling = (row, col + 1 - 2 * lax.rem(col, 2))
    tgt[...] = jnp.zeros_like(tgt)
    tgt[col, 0:2, :] = target_ref[...]
    barrier = pltpu.get_barrier_semaphore()
    near_peers = [near(0, dy, flip) for dy, flip in around] + [near(1, dy, flip) for dy, flip in around if flip]
    peers = near_peers + z_peers + c_peers
    for peer in peers:
        pl.semaphore_signal(barrier, inc=1, device_id=peer, device_id_type=MESH)

    blocks = 4
    panel = [panel_0, panel_1]

    def load(src, dst, k):
        pltpu.make_async_copy(src, dst, load_sem.at[k]).start()

    def load_column(k):
        for t in range(blocks):
            load(panel_hbm.at[pl.ds(t * B, B), pl.ds(k * B, B)], panel[k].at[t], k)

    def wait_load(ref, k):
        pltpu.make_async_copy(ref, ref, load_sem.at[k]).wait()

    def rows_of_part(q):
        return pl.ds(q * CH, CH)

    def send(src, dst, q, stage, peer):
        pltpu.make_async_remote_copy(
            src_ref=src, dst_ref=dst, send_sem=send_sem.at[q, stage], recv_sem=recv_sem.at[q, stage],
            device_id=peer, device_id_type=MESH,
        ).start()

    def arrived(ref, sem):
        pltpu.make_async_copy(ref, ref, sem).wait()

    def spread(q):
        for dy, flip in around:
            send(x_send.at[near_rows(q, dy, flip)], near_recv.at[q, dy * 2 + flip], q, 0, near(q, dy, flip))

    def reduce_near(q):
        arrived(near_recv.at[q, pl.ds(1, 7)], recv_sem.at[q, 0])
        total = x_send[near_rows(q, 0, 0), :]
        for d in range(1, 8):
            total = total + near_recv[q, d]
        z_send[q] = total
        for d, peer in zip(along, z_peers):
            send(z_send.at[q], z_recv.at[q, d // 2], q, 1, peer)

    def reduce_along(q):
        arrived(z_recv.at[q, pl.ds(1, 3)], recv_sem.at[q, 1])
        mine_here = near_rows(q, 0, 0)
        got[mine_here, :] = (z_send[q] + z_recv[q, 1]) + (z_recv[q, 2] + z_recv[q, 3])
        piece = got.at[mine_here]
        for dy, flip in around:
            send(piece, piece, q, 2, near(q, dy, flip))

    def gather(q):
        arrived(near_recv.at[q, pl.ds(1, 7)], recv_sem.at[q, 2])

    def across(src, dst, sem, q, peer):
        pltpu.make_async_remote_copy(
            src_ref=src, dst_ref=dst, send_sem=sem.at[0, q], recv_sem=sem.at[1, q],
            device_id=peer, device_id_type=MESH,
        ).start()

    def middle_out(q):
        rows = rows_of_part(q)
        for other in x_cols:
            across(got.at[rows], middle.at[col, rows], x_sem, q, (row, other))
        across(got.at[rows], middle.at[col, rows], core_sem, q, sibling)
        middle[col, rows, :] = got[rows, :]

    def middle_on(q):
        rows = rows_of_part(q)
        arrived(middle.at[pl.ds(0, 3), rows], x_sem.at[1, q])
        for other in x_cols:
            across(middle.at[other, rows], middle.at[other, rows], pass_sem, q, sibling)

    def middle_in(q):
        rows = rows_of_part(q)
        arrived(middle.at[0, rows], core_sem.at[1, q])
        arrived(middle.at[pl.ds(0, 3), rows], pass_sem.at[1, q])

    parts_m, parts_0, parts_1 = PARTS_M, PARTS_0, PARTS_1
    pl.semaphore_wait(barrier, len(peers))
    for q in parts_m + parts_0 + parts_1:
        spread(q)
    for t in range(blocks):
        load(rhs_hbm.at[pl.ds(t * B, B)], state.at[t], 2)
    load_column(0)
    load_column(1)
    for peer in c_peers:
        pltpu.make_async_remote_copy(
            src_ref=tgt.at[col], dst_ref=tgt.at[col], send_sem=tgt_sem.at[0], recv_sem=tgt_sem.at[1],
            device_id=peer, device_id_type=MESH,
        ).start()
    for q in parts_m + parts_0:
        reduce_near(q)
    for q in parts_m:
        reduce_along(q)
    for q in parts_1[:2]:
        reduce_near(q)
    for q in parts_m:
        gather(q)
        middle_out(q)
    for q in parts_1[2:]:
        reduce_near(q)
    for q in parts_0 + parts_1:
        reduce_along(q)
    for q in parts_m:
        middle_on(q)
    wait_load(state, 2)
    wait_load(panel_0, 0)
    wait_load(panel_1, 1)
    for q in parts_0:
        gather(q)

    first_rows = pl.ds(parts_0[0] * CH, B)

    def apply_first(t):
        state[t] = state[t] - dot(panel_0[t], got[first_rows, :])

    def apply_second(t):
        value = state[t] - dot(panel_1[t], second[...])
        value = jnp.where(slot_ref[1] == row * blocks + t, second_wide[...], value)
        value = jnp.where(slot_ref[0] == row * blocks + t, got[first_rows, :].astype(F32), value)
        state[t] = value

    def mean_weights():
        rest = jnp.concatenate([tgt[d] for d in range(NC)], axis=1)
        parts = []
        for _ in range(3):
            parts.append(rest.astype(BF16).astype(F32))
            rest = rest - parts[-1]
        return jnp.concatenate(parts + [jnp.zeros_like(rest)], axis=0).astype(BF16)

    def mean_terms(found, k):
        return found[k : k + 1] + found[8 + k : 9 + k] + found[16 + k : 17 + k]

    for t in range(blocks):
        apply_first(t)
    arrived(tgt.at[pl.ds(0, NC - 1)], tgt_sem.at[1])
    weights = mean_weights()
    mean = mean_terms(dot(weights, got[first_rows, :]), 0)
    for q in parts_1:
        gather(q)
    for q in parts_m:
        middle_in(q)
    for b in range(NCH):
        rows = rows_of_part(b)
        wide = jnp.concatenate(
            [middle[j, rows_of_part(b // 2), pl.ds(128 * (b % 2), 128)] for j in range(NC)], axis=1
        )
        x = got[rows_of_part(parts_1[b]), :].astype(F32) - dot(wide, got[first_rows, :])
        second_wide[rows, :] = x
        second[rows, :] = x.astype(BF16)
    for t in range(blocks):
        apply_second(t)
    hi, lo = split(second_wide[...])
    mean_ref[...] = (mean + mean_terms(dot(weights, hi) + dot(weights, lo), 1)).reshape(W)

    for q in range(PARTS):
        for stage, sent in enumerate((near_recv.at[q, pl.ds(1, 7)], z_recv.at[q, pl.ds(1, 3)], near_recv.at[q, pl.ds(1, 7)])):
            arrived(sent, send_sem.at[q, stage])
    for q in parts_m:
        rows = rows_of_part(q)
        arrived(middle.at[pl.ds(0, 3), rows], x_sem.at[0, q])
        arrived(middle.at[0, rows], core_sem.at[0, q])
        arrived(middle.at[pl.ds(0, 3), rows], pass_sem.at[0, q])
    arrived(tgt.at[pl.ds(0, NC - 1)], tgt_sem.at[0])


def per_device(panel, rhs, block_slot, target):
    rows, width = rhs.shape
    piece = (PIECE, W)
    ready = pl.pallas_call(
        prepare,
        out_shape=pltpu.VMEM((PARTS * CH, W), BF16),
        in_specs=[
            pl.BlockSpec(memory_space=pltpu.SMEM),
            pl.BlockSpec(memory_space=pl.ANY),
            pl.BlockSpec(memory_space=pl.ANY),
        ],
        out_specs=pl.BlockSpec(memory_space=pltpu.VMEM),
        scratch_shapes=[
            pltpu.VMEM((B, CH), BF16),
            pltpu.VMEM((6, CH, CH), BF16),
            pltpu.VMEM((B, W), F32),
            pltpu.VMEM((B, 128), BF16),
            pltpu.VMEM((NCH, CH, CH), BF16),
            pltpu.VMEM((NCH, CH, CH), BF16),
            pltpu.SemaphoreType.DMA((4,)),
        ],
        compiler_params=pltpu.CompilerParams(vmem_limit_bytes=58 * 2**20),
        name="prepare",
    )(block_slot, panel, rhs)
    ready = pltpu.with_memory_space_constraint(ready, pltpu.VMEM)
    out, mean = pl.pallas_call(
        kernel,
        out_shape=(pltpu.VMEM((rows // B, B, width), F32), jax.ShapeDtypeStruct((width,), F32)),
        in_specs=[
            pl.BlockSpec(memory_space=pltpu.SMEM),
            pl.BlockSpec(memory_space=pltpu.VMEM),
            pl.BlockSpec(memory_space=pltpu.VMEM),
            pl.BlockSpec(memory_space=pl.ANY),
            pl.BlockSpec(memory_space=pl.ANY),
        ],
        out_specs=(pl.BlockSpec(memory_space=pltpu.VMEM), pl.BlockSpec(memory_space=pltpu.VMEM)),
        scratch_shapes=[
            pltpu.VMEM((4, B, B), BF16),
            pltpu.VMEM((4, B, B), BF16),
            pltpu.VMEM((B, W), BF16),
            pltpu.VMEM((B, W), F32),
            pltpu.VMEM((PARTS, 8) + piece, BF16),
            pltpu.VMEM((PARTS,) + piece, BF16),
            pltpu.VMEM((PARTS, 4) + piece, BF16),
            pltpu.VMEM((PARTS * CH, W), BF16),
            pltpu.VMEM((NC, 2 * CH, W), BF16),
            pltpu.VMEM((NC, 8, 128), F32),
            pltpu.SemaphoreType.DMA((3,)),
            pltpu.SemaphoreType.DMA((PARTS, 3)),
            pltpu.SemaphoreType.DMA((PARTS, 3)),
            pltpu.SemaphoreType.DMA((2, 2)),
            pltpu.SemaphoreType.DMA((2, 2)),
            pltpu.SemaphoreType.DMA((2, 2)),
            pltpu.SemaphoreType.DMA((2,)),
        ],
        compiler_params=pltpu.CompilerParams(
            collective_id=0, has_side_effects=True, vmem_limit_bytes=56 * 2**20
        ),
        name="substitute",
    )(block_slot, target, ready, panel, rhs)
    return out.reshape(rows, width), mean


def solution(mesh):
    return jax.shard_map(
        per_device,
        mesh=mesh,
        in_specs=(P("row", None), P("row", "col"), P(), P(None, "col")),
        out_specs=(P("row", "col"), P("col")),
        check_vma=False,
    )
```

```python
import functools

import jax
import jax.numpy as jnp
from jax import lax
from jax.experimental import pallas as pl
from jax.experimental.pallas import tpu as pltpu
from jax.sharding import PartitionSpec as P

B = 1024
W = 256
NY, NZ, NC = 4, 8, 8
CH = 256
NCH = B // CH
BASE = 16
PIECE = CH // 8
F32, BF16 = jnp.float32, jnp.bfloat16
MESH = pl.DeviceIdType.MESH


def dot(a, b):
    return jnp.dot(a, b, preferred_element_type=F32)


def split(x):
    hi = x.astype(BF16)
    return hi, (x - hi.astype(F32)).astype(BF16)


def iota(shape, dim):
    return lax.broadcasted_iota(jnp.int32, shape, dim)


def spread_matrix():
    shape = (128, BASE * 128)
    lane = iota(shape, 1)
    return jnp.where(iota(shape, 0) == (lane % 128) // BASE * BASE + lane // 128, 1.0, 0.0).astype(BF16)


def invert_small(blocks, spread):
    groups = len(blocks)
    lane = iota((BASE, 128), 1)
    packed = []
    for block in blocks:
        wide = block.astype(F32)
        acc = jnp.zeros((BASE, 128), F32)
        for b in range(128 // BASE):
            acc = jnp.where(lane // BASE == b, wide[BASE * b : BASE * (b + 1)], acc)
        packed.append(acc)
    packed = jnp.concatenate(packed, axis=0).astype(BF16)
    factors = dot(packed, spread)
    part = [factors[:, 128 * j : 128 * (j + 1)].reshape(groups, BASE, 128) for j in range(BASE)]
    row = iota((groups, BASE, 128), 1)
    diag = part[0]
    for j in range(1, BASE):
        diag = jnp.where(row == j, part[j], diag)
    scale = 1.0 / diag
    x = jnp.where(iota((groups, BASE, 128), 2) % BASE == row, scale, 0.0)
    for j in range(BASE - 1):
        factor = jnp.where(row > j, part[j] * scale, 0.0)
        x = x - factor * x[:, j : j + 1, :]
    return [x[g] for g in range(groups)]


def join_inverses(diag_block):
    groups = B // 128
    spread = spread_matrix()
    blocks = [diag_block(g) for g in range(groups)]
    small = invert_small(blocks, spread)
    r, c = iota((128, 128), 0), iota((128, 128), 1)
    inverses = []
    for g in range(groups):
        tiled = jnp.concatenate([small[g]] * (128 // BASE), axis=0)
        inverses.append(jnp.where(r // BASE == c // BASE, tiled, 0.0))
    size = BASE
    while size < 128:
        odd = [slice(i, i + size) for i in range(size, 128, 2 * size)]
        mask = (c // size == r // size - 1) & ((r // size) % 2 == 1)
        off = [rows_of(jnp.where(mask, block, jnp.zeros_like(block)), odd) for block in blocks]
        inverses = joined(inverses, off, odd)
        size *= 2
    return inverses


def rows_of(x, parts):
    return jnp.concatenate([x[p] for p in parts], axis=0)


def joined(inverses, off, odd):
    size = odd[0].stop - odd[0].start
    parts = [split(x) for x in inverses]
    low = [(rows_of(hi, odd), rows_of(lo, odd)) for hi, lo in parts]
    t = [split(dot(jnp.concatenate([e, e], axis=1), jnp.concatenate(p, axis=0))) for e, p in zip(off, parts)]

    def spread_rows(x):
        gap = jnp.zeros((size, x.shape[1]), x.dtype)
        return jnp.concatenate([v for i in range(len(odd)) for v in (gap, x[size * i : size * (i + 1)])], axis=0)

    t = [(spread_rows(hi), spread_rows(lo)) for hi, lo in t]
    u = [
        dot(jnp.concatenate([p[0], p[1]], axis=1), jnp.concatenate([q[0], q[0]], axis=0)) for p, q in zip(low, t)
    ]
    v = [dot(p[0], q[1]) for p, q in zip(low, t)]
    out = []
    for x, y, w in zip(inverses, u, v):
        y = y + w
        pieces = []
        for i, p in enumerate(odd):
            pieces += [x[p.start - size : p.start], x[p] - y[size * i : size * (i + 1)]]
        out.append(jnp.concatenate(pieces, axis=0))
    return out


def whole_inverses(inverses, corners):
    parts = [split(x) for x in inverses]
    t = [
        split(dot(jnp.concatenate([e, e], axis=1), jnp.concatenate(parts[2 * b], axis=0)))
        for b, e in enumerate(corners)
    ]
    u = [
        dot(jnp.concatenate(parts[2 * b + 1], axis=1), jnp.concatenate([q[0], q[0]], axis=0)) for b, q in enumerate(t)
    ]
    v = [dot(parts[2 * b + 1][0], q[1]) for b, q in enumerate(t)]
    gap = jnp.zeros((128, 128), BF16)
    out = []
    for b in range(len(corners)):
        low = split(-(u[b] + v[b]))
        out.append(
            [
                jnp.concatenate(
                    [
                        jnp.concatenate([parts[2 * b][i], gap], axis=1),
                        jnp.concatenate([low[i], parts[2 * b + 1][i]], axis=1),
                    ],
                    axis=0,
                )
                for i in range(2)
            ]
        )
    return out


def kernel(
    slot_hbm, target_hbm, panel_hbm, rhs_hbm,
    state, panel_1, done, mean_ref, code,
    slot_ref, target_ref,
    panel_0, low_0, diag_0, diag_1, work, inv_hi, inv_lo, solved, x_send, near_recv, z_send, z_recv, tgt,
    load_sem, send_sem, recv_sem, tgt_send, tgt_recv,
):
    row, col = lax.axis_index("row"), lax.axis_index("col")
    y, z = row // NZ, row % NZ

    def half(c):
        return lax.rem(z + c % 2, 2)

    def near(c, dy, flip):
        step = flip * (1 - 2 * half(c))
        return (lax.rem(y + dy, NY) * NZ + lax.rem(z + step + NZ, NZ), col)

    def near_rows(c, dy, flip):
        slot = lax.rem(y + dy, NY) * 2 + half(c) + flip * (1 - 2 * half(c))
        return pl.ds(pl.multiple_of(c * CH + slot * PIECE, PIECE), PIECE)

    around = [(2, 1), (1, 1), (3, 1), (2, 0), (1, 0), (3, 0), (0, 1)]
    along = [4, 2, 6]
    z_peers = [(y * NZ + lax.rem(z + d, NZ), col) for d in along]
    c_peers = [(row, lax.rem(col + d, NC)) for d in range(1, NC)]
    tgt[...] = jnp.zeros_like(tgt)
    barrier = pltpu.get_barrier_semaphore()
    near_peers = [near(0, dy, flip) for dy, flip in around] + [near(1, dy, flip) for dy, flip in around if flip]
    peers = near_peers + z_peers + c_peers
    def load(src, dst, k):
        copy = pltpu.make_async_copy(src, dst, load_sem.at[k])
        copy.start()
        return copy

    blocks = 4
    panel, diag = [panel_0, panel_1], [diag_0, diag_1]

    def load_diag(k, sem):
        for t in range(blocks):
            for b in range(NCH):
                load(
                    panel_hbm.at[pl.ds(t * B + b * CH, CH), pl.ds(k * B + b * CH, CH)],
                    diag[k].at[t, pl.ds(b * CH, CH)],
                    sem,
                )

    def load_column(k, sem):
        for t in range(blocks):
            load(panel_hbm.at[pl.ds(t * B, B), pl.ds(k * B, B)], panel[k].at[t], sem)

    strip_at = [0, 3 * CH, 5 * CH]
    load_diag(0, 0)
    load(slot_hbm, slot_ref, 6)
    load(target_hbm, target_ref, 7)
    for peer in peers:
        pl.semaphore_signal(barrier, inc=1, device_id=peer, device_id_type=MESH)
    for t in range(blocks):
        load(rhs_hbm.at[pl.ds(t * B, B)], state.at[t], 1)
    for t in range(blocks):
        for a in range(NCH - 1):
            count = (NCH - 1 - a) * CH
            load(
                panel_hbm.at[pl.ds(t * B + (a + 1) * CH, count), pl.ds(a * CH, CH)],
                low_0.at[t, pl.ds(strip_at[a], count)],
                5,
            )

    pltpu.make_async_copy(slot_hbm, slot_ref, load_sem.at[6]).wait()
    mine = [slot_ref[0] // blocks == row, slot_ref[1] // blocks == row]
    local = [slot_ref[0] % blocks, slot_ref[1] % blocks]

    def wait_load(ref, k):
        pltpu.make_async_copy(ref, ref, load_sem.at[k]).wait()

    def invert(k):
        found = join_inverses(
            lambda g: diag[k][local[k], pl.ds(128 * g, 128), pl.ds(128 * (g % 2), 128)]
        )
        corners = [diag[k][local[k], pl.ds(CH * b + 128, 128), pl.ds(0, 128)] for b in range(NCH)]
        for b, (hi, lo) in enumerate(whole_inverses(found, corners)):
            inv_hi[b], inv_lo[b] = hi, lo

    def send(src, dst, k, c, stage, peer):
        pltpu.make_async_remote_copy(
            src_ref=src, dst_ref=dst, send_sem=send_sem.at[k, c, stage], recv_sem=recv_sem.at[k, c, stage],
            device_id=peer, device_id_type=MESH,
        ).start()

    def solve(k):
        his, los = [], []
        for b in range(NCH):
            part = work[pl.ds(b * CH, CH), :]
            for a in range(b):
                if k == 0:
                    tile = low_0[local[0], pl.ds(strip_at[a] + (b - a - 1) * CH, CH), :]
                else:
                    tile = panel_1[local[1], pl.ds(b * CH, CH), pl.ds(a * CH, CH)]
                part = part - (dot(tile, his[a]) + dot(tile, los[a]))
            hi, lo = split(part)
            ihi, ilo = inv_hi[b], inv_lo[b]
            x = dot(ihi, hi) + (dot(ihi, lo) + dot(ilo, hi))
            hi, lo = split(x)
            his.append(hi)
            los.append(lo)
            masked = jnp.where(mine[k], x, 0.0).astype(BF16)
            x_send[k, pl.ds(b * CH, CH), :] = masked
            if k == 0 and b == 0:
                pl.semaphore_wait(barrier, len(peers))
            for dy, flip in around:
                send(x_send.at[k, near_rows(b, dy, flip)], near_recv.at[k, b, dy * 2 + flip], k, b, 0, near(b, dy, flip))

    def arrived(ref, k, c, stage):
        pltpu.make_async_copy(ref, ref, recv_sem.at[k, c, stage]).wait()

    def reduce_near(k, c):
        arrived(near_recv.at[k, c, pl.ds(1, 7)], k, c, 0)
        total = x_send[k, near_rows(c, 0, 0), :]
        for d in range(1, 8):
            total = total + near_recv[k, c, d]
        z_send[k, c] = total
        for d, peer in zip(along, z_peers):
            send(z_send.at[k, c], z_recv.at[k, c, d // 2], k, c, 1, peer)

    def reduce_along(k, c):
        arrived(z_recv.at[k, c, pl.ds(1, 3)], k, c, 1)
        total = (z_send[k, c] + z_recv[k, c, 1]) + (z_recv[k, c, 2] + z_recv[k, c, 3])
        mine_here = near_rows(c, 0, 0)
        solved[k, mine_here, :] = total
        piece = solved.at[k, mine_here]
        for dy, flip in around:
            send(piece, piece, k, c, 2, near(c, dy, flip))

    def gather(k, c):
        arrived(near_recv.at[k, c, pl.ds(1, 7)], k, c, 2)

    wait_load(diag_0, 0)
    invert(0)
    wait_load(state, 1)
    work[...] = state[local[0]]
    wait_load(low_0, 5)
    solve(0)
    load_column(0, 2)
    load_diag(1, 3)
    load_column(1, 4)
    pltpu.make_async_copy(target_hbm, target_ref, load_sem.at[7]).wait()
    tgt[col, 0:2, :] = target_ref[...]
    for peer in c_peers:
        pltpu.make_async_remote_copy(
            src_ref=tgt.at[col], dst_ref=tgt.at[col], send_sem=tgt_send, recv_sem=tgt_recv,
            device_id=peer, device_id_type=MESH,
        ).start()
    for c in range(NCH):
        reduce_near(0, c)
    for c in range(NCH):
        reduce_along(0, c)
    wait_load(diag_1, 3)
    invert(1)
    work[...] = state[local[1]]
    wait_load(panel_0, 2)
    wait_load(panel_1, 4)
    for c in range(NCH):
        gather(0, c)
        work[...] = work[...] - dot(panel_0[local[1], :, pl.ds(c * CH, CH)], solved[0, pl.ds(c * CH, CH), :])
    solve(1)

    def apply_first(t):
        state[t] = state[t] - dot(panel_0[t], solved[0])

    def apply_second(t, c):
        part = pl.ds(c * CH, CH)
        state[t] = state[t] - dot(panel_1[t, :, part], solved[1, part, :])

    def mean_weights():
        rest = jnp.concatenate([tgt[d] for d in range(NC)], axis=1)
        parts = []
        for _ in range(3):
            parts.append(rest.astype(BF16).astype(F32))
            rest = rest - parts[-1]
        return jnp.concatenate(parts + [jnp.zeros_like(rest)], axis=0).astype(BF16)

    def mean_terms(weights, k):
        found = dot(weights, solved[k])
        return found[k : k + 1] + found[8 + k : 9 + k] + found[16 + k : 17 + k]

    apply_first(0)
    apply_first(1)
    for c in range(NCH):
        reduce_near(1, c)
    apply_first(2)
    for c in range(NCH):
        reduce_along(1, c)
    apply_first(3)
    pltpu.make_async_copy(tgt.at[pl.ds(0, NC - 1)], tgt.at[pl.ds(0, NC - 1)], tgt_recv).wait()
    weights = mean_weights()
    mean = mean_terms(weights, 0)
    done[0] = solved[0]
    kind = jnp.zeros((8, 128), jnp.int32)
    for t in range(blocks):
        here = [(slot_ref[i] == row * blocks + t).astype(jnp.int32) for i in range(2)]
        kind = jnp.where(iota((8, 128), 0) == t, 2 * here[0] + here[1], kind)
    code[...] = kind
    for c in range(NCH):
        gather(1, c)
        done[1, pl.ds(c * CH, CH), :] = solved[1, pl.ds(c * CH, CH), :]
        if c < NCH - 1:
            for t in range(blocks):
                apply_second(t, c)
    mean_ref[...] = (mean + mean_terms(weights, 1)).reshape(W)

    for k in range(2):
        for c in range(NCH):
            for stage, sent in enumerate((near_recv.at[k, c, pl.ds(1, 7)], z_recv.at[k, c, pl.ds(1, 3)], near_recv.at[k, c, pl.ds(1, 7)])):
                pltpu.make_async_copy(sent, sent, send_sem.at[k, c, stage]).wait()
    pltpu.make_async_copy(tgt.at[pl.ds(0, NC - 1)], tgt.at[pl.ds(0, NC - 1)], tgt_send).wait()


def finish(state, panel_1, done, mean, code, out_hbm, mean_hbm, stage, store_sem, mean_sem):
    blocks, rows = 4, B // 2
    last = pl.ds(B - CH, CH)
    pltpu.make_async_copy(mean, mean_hbm, mean_sem).start()
    for t in range(blocks):
        kind = jnp.broadcast_to(code[t : t + 1, :], (rows, 128))
        kind = jnp.concatenate([kind, kind], axis=1)
        for i in range(2):
            part = pl.ds(i * rows, rows)
            value = state[t, part, :] - dot(panel_1[t, part, last], done[1, last, :])
            value = jnp.where(kind == 1, done[1, part, :].astype(F32), value)
            stage[t, part, :] = jnp.where(kind == 2, done[0, part, :].astype(F32), value)
            pltpu.make_async_copy(
                stage.at[t, part], out_hbm.at[pl.ds(t * B + i * rows, rows)], store_sem.at[t, i]
            ).start()
    for t in range(blocks):
        for i in range(2):
            part = pl.ds(i * rows, rows)
            pltpu.make_async_copy(
                stage.at[t, part], out_hbm.at[pl.ds(t * B + i * rows, rows)], store_sem.at[t, i]
            ).wait()
    pltpu.make_async_copy(mean, mean_hbm, mean_sem).wait()


def per_device(panel, rhs, block_slot, target):
    rows, width = rhs.shape
    piece = (PIECE, W)
    held = pl.pallas_call(
        kernel,
        out_shape=(
            pltpu.VMEM((rows // B, B, width), F32),
            pltpu.VMEM((4, B, B), BF16),
            pltpu.VMEM((2, B, W), BF16),
            pltpu.VMEM((width,), F32),
            pltpu.VMEM((8, 128), jnp.int32),
        ),
        in_specs=[pl.BlockSpec(memory_space=pl.ANY)] * 4,
        out_specs=(pl.BlockSpec(memory_space=pltpu.VMEM),) * 5,
        scratch_shapes=[
            pltpu.SMEM((128,), jnp.int32),
            pltpu.VMEM((2, 128), F32),
            pltpu.VMEM((4, B, B), BF16),
            pltpu.VMEM((4, 6 * CH, CH), BF16),
            pltpu.VMEM((4, B, CH), BF16),
            pltpu.VMEM((4, B, CH), BF16),
            pltpu.VMEM((B, W), F32),
            pltpu.VMEM((NCH, CH, CH), BF16),
            pltpu.VMEM((NCH, CH, CH), BF16),
            pltpu.VMEM((2, B, W), BF16),
            pltpu.VMEM((2, B, W), BF16),
            pltpu.VMEM((2, NCH, 8) + piece, BF16),
            pltpu.VMEM((2, NCH) + piece, BF16),
            pltpu.VMEM((2, NCH, 4) + piece, BF16),
            pltpu.VMEM((NC, 8, 128), F32),
            pltpu.SemaphoreType.DMA((8,)),
            pltpu.SemaphoreType.DMA((2, NCH, 3)),
            pltpu.SemaphoreType.DMA((2, NCH, 3)),
            pltpu.SemaphoreType.DMA,
            pltpu.SemaphoreType.DMA,
        ],
        compiler_params=pltpu.CompilerParams(
            collective_id=0, has_side_effects=True, vmem_limit_bytes=44 * 2**20
        ),
        name="substitute",
    )(block_slot, target, panel, rhs)
    held = [pltpu.with_memory_space_constraint(v, pltpu.VMEM) for v in held]
    return pl.pallas_call(
        finish,
        out_shape=(jax.ShapeDtypeStruct((rows, width), F32), jax.ShapeDtypeStruct((width,), F32)),
        in_specs=[pl.BlockSpec(memory_space=pltpu.VMEM)] * 5,
        out_specs=(pl.BlockSpec(memory_space=pl.ANY),) * 2,
        scratch_shapes=[pltpu.VMEM((4, B, W), F32), pltpu.SemaphoreType.DMA((4, 2)), pltpu.SemaphoreType.DMA],
        compiler_params=pltpu.CompilerParams(vmem_limit_bytes=20 * 2**20),
        name="finish",
    )(*held)


def solution(mesh):
    return jax.shard_map(
        per_device,
        mesh=mesh,
        in_specs=(P("row", None), P("row", "col"), P(), P(None, "col")),
        out_specs=(P("row", "col"), P("col")),
        check_vma=False,
    )
```

```python
import functools

import jax
import jax.numpy as jnp
from jax import lax
from jax.experimental import pallas as pl
from jax.experimental.pallas import tpu as pltpu
from jax.sharding import PartitionSpec as P

B = 1024
W = 256
NY, NZ, NC = 4, 8, 8
CH = 256
NCH = B // CH
BASE = 16
PIECE = CH // 8
F32, BF16 = jnp.float32, jnp.bfloat16
MESH = pl.DeviceIdType.MESH


def dot(a, b):
    return jnp.dot(a, b, preferred_element_type=F32)


def split(x):
    hi = x.astype(BF16)
    return hi, (x - hi.astype(F32)).astype(BF16)


def iota(shape, dim):
    return lax.broadcasted_iota(jnp.int32, shape, dim)


def spread_matrix():
    shape = (128, BASE * 128)
    lane = iota(shape, 1)
    return jnp.where(iota(shape, 0) == (lane % 128) // BASE * BASE + lane // 128, 1.0, 0.0).astype(BF16)


def invert_small(blocks, spread):
    groups = len(blocks)
    lane = iota((BASE, 128), 1)
    packed = []
    for block in blocks:
        wide = block.astype(F32)
        acc = jnp.zeros((BASE, 128), F32)
        for b in range(128 // BASE):
            acc = jnp.where(lane // BASE == b, wide[BASE * b : BASE * (b + 1)], acc)
        packed.append(acc)
    packed = jnp.concatenate(packed, axis=0).astype(BF16)
    factors = dot(packed, spread)
    part = [factors[:, 128 * j : 128 * (j + 1)].reshape(groups, BASE, 128) for j in range(BASE)]
    row = iota((groups, BASE, 128), 1)
    diag = part[0]
    for j in range(1, BASE):
        diag = jnp.where(row == j, part[j], diag)
    scale = 1.0 / diag
    x = jnp.where(iota((groups, BASE, 128), 2) % BASE == row, scale, 0.0)
    for j in range(BASE - 1):
        factor = jnp.where(row > j, part[j] * scale, 0.0)
        x = x - factor * x[:, j : j + 1, :]
    return [x[g] for g in range(groups)]


def join_inverses(blocks, spread):
    groups = len(blocks)
    small = invert_small(blocks, spread)
    r, c = iota((128, 128), 0), iota((128, 128), 1)
    inverses = []
    for g in range(groups):
        tiled = jnp.concatenate([small[g]] * (128 // BASE), axis=0)
        inverses.append(jnp.where(r // BASE == c // BASE, tiled, 0.0))
    size = BASE
    while size < 128:
        odd = [slice(i, i + size) for i in range(size, 128, 2 * size)]
        mask = (c // size == r // size - 1) & ((r // size) % 2 == 1)
        off = [rows_of(jnp.where(mask, block, jnp.zeros_like(block)), odd) for block in blocks]
        inverses = joined(inverses, off, odd)
        size *= 2
    return inverses


def rows_of(x, parts):
    return jnp.concatenate([x[p] for p in parts], axis=0)


def joined(inverses, off, odd):
    size = odd[0].stop - odd[0].start
    parts = [split(x) for x in inverses]
    low = [(rows_of(hi, odd), rows_of(lo, odd)) for hi, lo in parts]
    t = [split(dot(jnp.concatenate([e, e], axis=1), jnp.concatenate(p, axis=0))) for e, p in zip(off, parts)]

    def spread_rows(x):
        gap = jnp.zeros((size, x.shape[1]), x.dtype)
        return jnp.concatenate([v for i in range(len(odd)) for v in (gap, x[size * i : size * (i + 1)])], axis=0)

    t = [(spread_rows(hi), spread_rows(lo)) for hi, lo in t]
    u = [
        dot(jnp.concatenate([p[0], p[1]], axis=1), jnp.concatenate([q[0], q[0]], axis=0)) for p, q in zip(low, t)
    ]
    v = [dot(p[0], q[1]) for p, q in zip(low, t)]
    out = []
    for x, y, w in zip(inverses, u, v):
        y = y + w
        pieces = []
        for i, p in enumerate(odd):
            pieces += [x[p.start - size : p.start], x[p] - y[size * i : size * (i + 1)]]
        out.append(jnp.concatenate(pieces, axis=0))
    return out


def whole_inverses(inverses, corners):
    parts = [split(x) for x in inverses]
    t = [
        split(dot(jnp.concatenate([e, e], axis=1), jnp.concatenate(parts[2 * b], axis=0)))
        for b, e in enumerate(corners)
    ]
    u = [
        dot(jnp.concatenate(parts[2 * b + 1], axis=1), jnp.concatenate([q[0], q[0]], axis=0)) for b, q in enumerate(t)
    ]
    v = [dot(parts[2 * b + 1][0], q[1]) for b, q in enumerate(t)]
    gap = jnp.zeros((128, 128), BF16)
    out = []
    for b in range(len(corners)):
        low = split(-(u[b] + v[b]))
        out.append(
            [
                jnp.concatenate(
                    [
                        jnp.concatenate([parts[2 * b][i], gap], axis=1),
                        jnp.concatenate([low[i], parts[2 * b + 1][i]], axis=1),
                    ],
                    axis=0,
                )
                for i in range(2)
            ]
        )
    return out


def kernel(
    slot_hbm, target_hbm, panel_hbm, rhs_hbm,
    state, panel_1, done, mean_ref, code,
    slot_ref, target_ref,
    spread_ref, panel_0, low_0, diag_a, diag_b, diag_1, work, inv_hi, inv_lo, solved, x_send, near_recv, z_send, z_recv, tgt,
    load_sem, send_sem, recv_sem, tgt_send, tgt_recv,
):
    row, col = lax.axis_index("row"), lax.axis_index("col")
    y, z = row // NZ, row % NZ

    def half(c):
        return lax.rem(z + c % 2, 2)

    def near(c, dy, flip):
        step = flip * (1 - 2 * half(c))
        return (lax.rem(y + dy, NY) * NZ + lax.rem(z + step + NZ, NZ), col)

    def near_rows(c, dy, flip):
        slot = lax.rem(y + dy, NY) * 2 + half(c) + flip * (1 - 2 * half(c))
        return pl.ds(pl.multiple_of(c * CH + slot * PIECE, PIECE), PIECE)

    around = [(2, 1), (1, 1), (3, 1), (2, 0), (1, 0), (3, 0), (0, 1)]
    along = [4, 2, 6]
    z_peers = [(y * NZ + lax.rem(z + d, NZ), col) for d in along]
    c_peers = [(row, lax.rem(col + d, NC)) for d in range(1, NC)]
    tgt[...] = jnp.zeros_like(tgt)
    barrier = pltpu.get_barrier_semaphore()
    near_peers = [near(0, dy, flip) for dy, flip in around] + [near(1, dy, flip) for dy, flip in around if flip]
    peers = near_peers + z_peers + c_peers
    def load(src, dst, k):
        copy = pltpu.make_async_copy(src, dst, load_sem.at[k])
        copy.start()
        return copy

    blocks = 4
    panel = [panel_0, panel_1]

    def load_diag(k, parts, dst, sem):
        for t in range(blocks):
            for i, b in enumerate(parts):
                load(
                    panel_hbm.at[pl.ds(t * B + b * CH, CH), pl.ds(k * B + b * CH, CH)],
                    dst.at[t, pl.ds(i * CH, CH)],
                    sem,
                )

    def load_column(k, sem):
        for t in range(blocks):
            load(panel_hbm.at[pl.ds(t * B, B), pl.ds(k * B, B)], panel[k].at[t], sem)

    strip_at = [0, 3 * CH, 5 * CH]
    load_diag(0, [0, 1], diag_a, 0)
    load(slot_hbm, slot_ref, 6)
    load(target_hbm, target_ref, 7)
    for peer in peers:
        pl.semaphore_signal(barrier, inc=1, device_id=peer, device_id_type=MESH)
    for t in range(blocks):
        load(rhs_hbm.at[pl.ds(t * B, B)], state.at[t], 1)
    load_diag(0, [2, 3], diag_b, 8)
    for t in range(blocks):
        for a in range(NCH - 1):
            count = (NCH - 1 - a) * CH
            load(
                panel_hbm.at[pl.ds(t * B + (a + 1) * CH, count), pl.ds(a * CH, CH)],
                low_0.at[t, pl.ds(strip_at[a], count)],
                5,
            )

    spread_ref[...] = spread_matrix()
    pltpu.make_async_copy(slot_hbm, slot_ref, load_sem.at[6]).wait()
    mine = [slot_ref[0] // blocks == row, slot_ref[1] // blocks == row]
    local = [slot_ref[0] % blocks, slot_ref[1] % blocks]

    def wait_load(ref, k):
        pltpu.make_async_copy(ref, ref, load_sem.at[k]).wait()

    def invert(k, parts):
        def diagonal(b, r, c):
            buf = diag_1 if k else (diag_a if b < 2 else diag_b)
            return buf[local[k], pl.ds((b if k else b % 2) * CH + r, 128), pl.ds(c, 128)]

        found = join_inverses([diagonal(b, r, r) for b in parts for r in (0, 128)], spread_ref[...])
        for b, (hi, lo) in zip(parts, whole_inverses(found, [diagonal(b, 128, 0) for b in parts])):
            inv_hi[b], inv_lo[b] = hi, lo

    def send(src, dst, k, c, stage, peer):
        pltpu.make_async_remote_copy(
            src_ref=src, dst_ref=dst, send_sem=send_sem.at[k, c, stage], recv_sem=recv_sem.at[k, c, stage],
            device_id=peer, device_id_type=MESH,
        ).start()

    def solve(k):
        his, los = [], []
        for b in range(NCH):
            if k == 0 and b == 1:
                wait_load(low_0, 5)
            if k == 0 and b == 2:
                wait_load(diag_b, 8)
                invert(0, [2, 3])
            rows, last = pl.ds(b * CH, CH), pl.ds(B - CH, CH)
            if k == 0:
                part = state[local[0], rows, :]
            else:
                part = work[rows, :] - dot(panel_0[local[1], rows, last], solved[0, last, :])
            for a in range(b):
                if k == 0:
                    tile = low_0[local[0], pl.ds(strip_at[a] + (b - a - 1) * CH, CH), :]
                else:
                    tile = panel_1[local[1], pl.ds(b * CH, CH), pl.ds(a * CH, CH)]
                part = part - (dot(tile, his[a]) + dot(tile, los[a]))
            hi, lo = split(part)
            ihi, ilo = inv_hi[b], inv_lo[b]
            x = dot(ihi, hi) + (dot(ihi, lo) + dot(ilo, hi))
            hi, lo = split(x)
            his.append(hi)
            los.append(lo)
            masked = jnp.where(mine[k], x, 0.0).astype(BF16)
            x_send[k, pl.ds(b * CH, CH), :] = masked
            if k == 0 and b == 0:
                pl.semaphore_wait(barrier, len(peers))
            for dy, flip in around:
                send(x_send.at[k, near_rows(b, dy, flip)], near_recv.at[k, b, dy * 2 + flip], k, b, 0, near(b, dy, flip))

    def arrived(ref, k, c, stage):
        pltpu.make_async_copy(ref, ref, recv_sem.at[k, c, stage]).wait()

    def reduce_near(k, c):
        arrived(near_recv.at[k, c, pl.ds(1, 7)], k, c, 0)
        total = x_send[k, near_rows(c, 0, 0), :]
        for d in range(1, 8):
            total = total + near_recv[k, c, d]
        z_send[k, c] = total
        for d, peer in zip(along, z_peers):
            send(z_send.at[k, c], z_recv.at[k, c, d // 2], k, c, 1, peer)

    def reduce_along(k, c):
        arrived(z_recv.at[k, c, pl.ds(1, 3)], k, c, 1)
        total = (z_send[k, c] + z_recv[k, c, 1]) + (z_recv[k, c, 2] + z_recv[k, c, 3])
        mine_here = near_rows(c, 0, 0)
        solved[k, mine_here, :] = total
        piece = solved.at[k, mine_here]
        for dy, flip in around:
            send(piece, piece, k, c, 2, near(c, dy, flip))

    def gather(k, c):
        arrived(near_recv.at[k, c, pl.ds(1, 7)], k, c, 2)

    wait_load(diag_a, 0)
    invert(0, [0, 1])
    wait_load(state, 1)
    solve(0)
    load_column(0, 2)
    load_diag(1, range(NCH), diag_1, 3)
    load_column(1, 4)
    pltpu.make_async_copy(target_hbm, target_ref, load_sem.at[7]).wait()
    tgt[col, 0:2, :] = target_ref[...]
    for peer in c_peers:
        pltpu.make_async_remote_copy(
            src_ref=tgt.at[col], dst_ref=tgt.at[col], send_sem=tgt_send, recv_sem=tgt_recv,
            device_id=peer, device_id_type=MESH,
        ).start()
    for c in range(NCH):
        reduce_near(0, c)
    for c in range(NCH):
        reduce_along(0, c)
    wait_load(diag_1, 3)
    invert(1, range(NCH))
    work[...] = state[local[1]]
    wait_load(panel_0, 2)
    wait_load(panel_1, 4)
    for c in range(NCH):
        gather(0, c)
        if c == NCH - 1:
            break
        work[...] = work[...] - dot(panel_0[local[1], :, pl.ds(c * CH, CH)], solved[0, pl.ds(c * CH, CH), :])
    solve(1)

    def apply_first(t):
        state[t] = state[t] - dot(panel_0[t], solved[0])

    def apply_second(t, c):
        part = pl.ds(c * CH, CH)
        state[t] = state[t] - dot(panel_1[t, :, part], solved[1, part, :])

    def mean_weights():
        rest = jnp.concatenate([tgt[d] for d in range(NC)], axis=1)
        parts = []
        for _ in range(3):
            parts.append(rest.astype(BF16).astype(F32))
            rest = rest - parts[-1]
        return jnp.concatenate(parts + [jnp.zeros_like(rest)], axis=0).astype(BF16)

    def mean_terms(weights, k):
        found = dot(weights, solved[k])
        return found[k : k + 1] + found[8 + k : 9 + k] + found[16 + k : 17 + k]

    apply_first(0)
    apply_first(1)
    for c in range(NCH):
        reduce_near(1, c)
    apply_first(2)
    for c in range(NCH):
        reduce_along(1, c)
    apply_first(3)
    pltpu.make_async_copy(tgt.at[pl.ds(0, NC - 1)], tgt.at[pl.ds(0, NC - 1)], tgt_recv).wait()
    weights = mean_weights()
    mean = mean_terms(weights, 0)
    done[0] = solved[0]
    kind = jnp.zeros((8, 128), jnp.int32)
    for t in range(blocks):
        here = [(slot_ref[i] == row * blocks + t).astype(jnp.int32) for i in range(2)]
        kind = jnp.where(iota((8, 128), 0) == t, 2 * here[0] + here[1], kind)
    code[...] = kind
    for c in range(NCH):
        gather(1, c)
        done[1, pl.ds(c * CH, CH), :] = solved[1, pl.ds(c * CH, CH), :]
        if c < NCH - 1:
            for t in range(blocks):
                apply_second(t, c)
    mean_ref[...] = (mean + mean_terms(weights, 1)).reshape(W)

    for k in range(2):
        for c in range(NCH):
            for stage, sent in enumerate((near_recv.at[k, c, pl.ds(1, 7)], z_recv.at[k, c, pl.ds(1, 3)], near_recv.at[k, c, pl.ds(1, 7)])):
                pltpu.make_async_copy(sent, sent, send_sem.at[k, c, stage]).wait()
    pltpu.make_async_copy(tgt.at[pl.ds(0, NC - 1)], tgt.at[pl.ds(0, NC - 1)], tgt_send).wait()


def finish(state, panel_1, done, mean, code, out_hbm, mean_hbm, stage, store_sem, mean_sem):
    blocks, rows = 4, B // 2
    last = pl.ds(B - CH, CH)
    pltpu.make_async_copy(mean, mean_hbm, mean_sem).start()
    for t in range(blocks):
        kind = jnp.broadcast_to(code[t : t + 1, :], (rows, 128))
        kind = jnp.concatenate([kind, kind], axis=1)
        for i in range(2):
            part = pl.ds(i * rows, rows)
            value = state[t, part, :] - dot(panel_1[t, part, last], done[1, last, :])
            value = jnp.where(kind == 1, done[1, part, :].astype(F32), value)
            stage[t, part, :] = jnp.where(kind == 2, done[0, part, :].astype(F32), value)
            pltpu.make_async_copy(
                stage.at[t, part], out_hbm.at[pl.ds(t * B + i * rows, rows)], store_sem.at[t, i]
            ).start()
    for t in range(blocks):
        for i in range(2):
            part = pl.ds(i * rows, rows)
            pltpu.make_async_copy(
                stage.at[t, part], out_hbm.at[pl.ds(t * B + i * rows, rows)], store_sem.at[t, i]
            ).wait()
    pltpu.make_async_copy(mean, mean_hbm, mean_sem).wait()


def per_device(panel, rhs, block_slot, target):
    rows, width = rhs.shape
    piece = (PIECE, W)
    held = pl.pallas_call(
        kernel,
        out_shape=(
            pltpu.VMEM((rows // B, B, width), F32),
            pltpu.VMEM((4, B, B), BF16),
            pltpu.VMEM((2, B, W), BF16),
            pltpu.VMEM((width,), F32),
            pltpu.VMEM((8, 128), jnp.int32),
        ),
        in_specs=[pl.BlockSpec(memory_space=pl.ANY)] * 4,
        out_specs=(pl.BlockSpec(memory_space=pltpu.VMEM),) * 5,
        scratch_shapes=[
            pltpu.SMEM((128,), jnp.int32),
            pltpu.VMEM((2, 128), F32),
            pltpu.VMEM((128, BASE * 128), BF16),
            pltpu.VMEM((4, B, B), BF16),
            pltpu.VMEM((4, 6 * CH, CH), BF16),
            pltpu.VMEM((4, 2 * CH, CH), BF16),
            pltpu.VMEM((4, 2 * CH, CH), BF16),
            pltpu.VMEM((4, B, CH), BF16),
            pltpu.VMEM((B, W), F32),
            pltpu.VMEM((NCH, CH, CH), BF16),
            pltpu.VMEM((NCH, CH, CH), BF16),
            pltpu.VMEM((2, B, W), BF16),
            pltpu.VMEM((2, B, W), BF16),
            pltpu.VMEM((2, NCH, 8) + piece, BF16),
            pltpu.VMEM((2, NCH) + piece, BF16),
            pltpu.VMEM((2, NCH, 4) + piece, BF16),
            pltpu.VMEM((NC, 8, 128), F32),
            pltpu.SemaphoreType.DMA((9,)),
            pltpu.SemaphoreType.DMA((2, NCH, 3)),
            pltpu.SemaphoreType.DMA((2, NCH, 3)),
            pltpu.SemaphoreType.DMA,
            pltpu.SemaphoreType.DMA,
        ],
        compiler_params=pltpu.CompilerParams(
            collective_id=0, has_side_effects=True, vmem_limit_bytes=44 * 2**20
        ),
        name="substitute",
    )(block_slot, target, panel, rhs)
    held = [pltpu.with_memory_space_constraint(v, pltpu.VMEM) for v in held]
    return pl.pallas_call(
        finish,
        out_shape=(jax.ShapeDtypeStruct((rows, width), F32), jax.ShapeDtypeStruct((width,), F32)),
        in_specs=[pl.BlockSpec(memory_space=pltpu.VMEM)] * 5,
        out_specs=(pl.BlockSpec(memory_space=pl.ANY),) * 2,
        scratch_shapes=[pltpu.VMEM((4, B, W), F32), pltpu.SemaphoreType.DMA((4, 2)), pltpu.SemaphoreType.DMA],
        compiler_params=pltpu.CompilerParams(vmem_limit_bytes=20 * 2**20),
        name="finish",
    )(*held)


def solution(mesh):
    return jax.shard_map(
        per_device,
        mesh=mesh,
        in_specs=(P("row", None), P("row", "col"), P(), P(None, "col")),
        out_specs=(P("row", "col"), P("col")),
        check_vma=False,
    )
```

```python
import functools

import jax
import jax.numpy as jnp
from jax import lax
from jax.experimental import pallas as pl
from jax.experimental.pallas import tpu as pltpu
from jax.sharding import PartitionSpec as P

B = 1024
W = 256
NY, NZ, NC = 4, 8, 8
CH = 256
NCH = B // CH
BASE = 16
PIECE = CH // 8
F32, BF16 = jnp.float32, jnp.bfloat16
MESH = pl.DeviceIdType.MESH


def dot(a, b):
    return jnp.dot(a, b, preferred_element_type=F32)


def split(x):
    hi = x.astype(BF16)
    return hi, (x - hi.astype(F32)).astype(BF16)


def iota(shape, dim):
    return lax.broadcasted_iota(jnp.int32, shape, dim)


def spread_matrix():
    shape = (128, BASE * 128)
    lane = iota(shape, 1)
    return jnp.where(iota(shape, 0) == (lane % 128) // BASE * BASE + lane // 128, 1.0, 0.0).astype(BF16)


def invert_small(blocks, spread):
    groups = len(blocks)
    lane = iota((BASE, 128), 1)
    packed = []
    for block in blocks:
        wide = block.astype(F32)
        acc = jnp.zeros((BASE, 128), F32)
        for b in range(128 // BASE):
            acc = jnp.where(lane // BASE == b, wide[BASE * b : BASE * (b + 1)], acc)
        packed.append(acc)
    packed = jnp.concatenate(packed, axis=0).astype(BF16)
    factors = dot(packed, spread)
    part = [factors[:, 128 * j : 128 * (j + 1)].reshape(groups, BASE, 128) for j in range(BASE)]
    row = iota((groups, BASE, 128), 1)
    diag = part[0]
    for j in range(1, BASE):
        diag = jnp.where(row == j, part[j], diag)
    scale = 1.0 / diag
    x = jnp.where(iota((groups, BASE, 128), 2) % BASE == row, scale, 0.0)
    for j in range(BASE - 1):
        factor = jnp.where(row > j, part[j] * scale, 0.0)
        x = x - factor * x[:, j : j + 1, :]
    return [x[g] for g in range(groups)]


def join_inverses(blocks, spread):
    groups = len(blocks)
    small = invert_small(blocks, spread)
    r, c = iota((128, 128), 0), iota((128, 128), 1)
    inverses = []
    for g in range(groups):
        tiled = jnp.concatenate([small[g]] * (128 // BASE), axis=0)
        inverses.append(jnp.where(r // BASE == c // BASE, tiled, 0.0))
    size = BASE
    while size < 128:
        odd = [slice(i, i + size) for i in range(size, 128, 2 * size)]
        mask = (c // size == r // size - 1) & ((r // size) % 2 == 1)
        off = [rows_of(jnp.where(mask, block, jnp.zeros_like(block)), odd) for block in blocks]
        inverses = joined(inverses, off, odd)
        size *= 2
    return inverses


def rows_of(x, parts):
    return jnp.concatenate([x[p] for p in parts], axis=0)


def joined(inverses, off, odd):
    size = odd[0].stop - odd[0].start
    parts = [split(x) for x in inverses]
    low = [(rows_of(hi, odd), rows_of(lo, odd)) for hi, lo in parts]
    t = [split(dot(jnp.concatenate([e, e], axis=1), jnp.concatenate(p, axis=0))) for e, p in zip(off, parts)]

    def spread_rows(x):
        gap = jnp.zeros((size, x.shape[1]), x.dtype)
        return jnp.concatenate([v for i in range(len(odd)) for v in (gap, x[size * i : size * (i + 1)])], axis=0)

    t = [(spread_rows(hi), spread_rows(lo)) for hi, lo in t]
    u = [
        dot(jnp.concatenate([p[0], p[1]], axis=1), jnp.concatenate([q[0], q[0]], axis=0)) for p, q in zip(low, t)
    ]
    v = [dot(p[0], q[1]) for p, q in zip(low, t)]
    out = []
    for x, y, w in zip(inverses, u, v):
        y = y + w
        pieces = []
        for i, p in enumerate(odd):
            pieces += [x[p.start - size : p.start], x[p] - y[size * i : size * (i + 1)]]
        out.append(jnp.concatenate(pieces, axis=0))
    return out


def whole_inverses(inverses, corners):
    parts = [split(x) for x in inverses]
    t = [
        split(dot(jnp.concatenate([e, e], axis=1), jnp.concatenate(parts[2 * b], axis=0)))
        for b, e in enumerate(corners)
    ]
    u = [
        dot(jnp.concatenate(parts[2 * b + 1], axis=1), jnp.concatenate([q[0], q[0]], axis=0)) for b, q in enumerate(t)
    ]
    v = [dot(parts[2 * b + 1][0], q[1]) for b, q in enumerate(t)]
    gap = jnp.zeros((128, 128), BF16)
    out = []
    for b in range(len(corners)):
        low = split(-(u[b] + v[b]))
        out.append(
            [
                jnp.concatenate(
                    [
                        jnp.concatenate([parts[2 * b][i], gap], axis=1),
                        jnp.concatenate([low[i], parts[2 * b + 1][i]], axis=1),
                    ],
                    axis=0,
                )
                for i in range(2)
            ]
        )
    return out


def kernel(
    slot_hbm, target_hbm, panel_hbm, rhs_hbm,
    state, panel_1, done, mean_ref, code,
    slot_ref, target_ref,
    spread_ref, panel_0, low_0, diag_a, diag_b, diag_1, work, inv_hi, inv_lo, solved, x_send, near_recv, z_send, z_recv, tgt,
    load_sem, send_sem, recv_sem, tgt_send, tgt_recv,
):
    row, col = lax.axis_index("row"), lax.axis_index("col")
    y, z = row // NZ, row % NZ

    def half(c):
        return lax.rem(z, 2)

    def near(c, dy, flip):
        step = flip * (1 - 2 * half(c))
        return (lax.rem(y + dy, NY) * NZ + lax.rem(z + step + NZ, NZ), col)

    def near_rows(c, dy, flip):
        slot = lax.rem(y + dy, NY) * 2 + half(c) + flip * (1 - 2 * half(c))
        return pl.ds(pl.multiple_of(c * CH + slot * PIECE, PIECE), PIECE)

    around = [(2, 1), (1, 1), (3, 1), (2, 0), (1, 0), (3, 0), (0, 1)]
    along = [4, 2, 6]
    z_peers = [(y * NZ + lax.rem(z + d, NZ), col) for d in along]
    c_peers = [(row, lax.rem(col + d, NC)) for d in range(1, NC)]
    tgt[...] = jnp.zeros_like(tgt)
    barrier = pltpu.get_barrier_semaphore()
    near_peers = [near(0, dy, flip) for dy, flip in around]
    peers = near_peers + z_peers + c_peers
    def load(src, dst, k):
        copy = pltpu.make_async_copy(src, dst, load_sem.at[k])
        copy.start()
        return copy

    blocks = 4
    panel = [panel_0, panel_1]

    def load_diag(k, parts, dst, sem):
        for t in range(blocks):
            for i, b in enumerate(parts):
                load(
                    panel_hbm.at[pl.ds(t * B + b * CH, CH), pl.ds(k * B + b * CH, CH)],
                    dst.at[t, pl.ds(i * CH, CH)],
                    sem,
                )

    def load_column(k, sem):
        for t in range(blocks):
            load(panel_hbm.at[pl.ds(t * B, B), pl.ds(k * B, B)], panel[k].at[t], sem)

    strip_at = [0, 3 * CH, 5 * CH]
    load_diag(0, [0, 1], diag_a, 0)
    load(slot_hbm, slot_ref, 6)
    load(target_hbm, target_ref, 7)
    for peer in peers:
        pl.semaphore_signal(barrier, inc=1, device_id=peer, device_id_type=MESH)
    for t in range(blocks):
        load(rhs_hbm.at[pl.ds(t * B, B)], state.at[t], 1)
    load_diag(0, [2, 3], diag_b, 8)
    for t in range(blocks):
        for a in range(NCH - 1):
            count = (NCH - 1 - a) * CH
            load(
                panel_hbm.at[pl.ds(t * B + (a + 1) * CH, count), pl.ds(a * CH, CH)],
                low_0.at[t, pl.ds(strip_at[a], count)],
                5,
            )

    spread_ref[...] = spread_matrix()
    pltpu.make_async_copy(slot_hbm, slot_ref, load_sem.at[6]).wait()
    mine = [slot_ref[0] // blocks == row, slot_ref[1] // blocks == row]
    local = [slot_ref[0] % blocks, slot_ref[1] % blocks]

    def wait_load(ref, k):
        pltpu.make_async_copy(ref, ref, load_sem.at[k]).wait()

    def invert(k, parts):
        def diagonal(b, r, c):
            buf = diag_1 if k else (diag_a if b < 2 else diag_b)
            return buf[local[k], pl.ds((b if k else b % 2) * CH + r, 128), pl.ds(c, 128)]

        found = join_inverses([diagonal(b, r, r) for b in parts for r in (0, 128)], spread_ref[...])
        for b, (hi, lo) in zip(parts, whole_inverses(found, [diagonal(b, 128, 0) for b in parts])):
            inv_hi[b], inv_lo[b] = hi, lo

    def send(src, dst, k, c, stage, peer):
        pltpu.make_async_remote_copy(
            src_ref=src, dst_ref=dst, send_sem=send_sem.at[k, c, stage], recv_sem=recv_sem.at[k, c, stage],
            device_id=peer, device_id_type=MESH,
        ).start()

    def solve(k):
        his, los = [], []
        for b in range(NCH):
            if k == 0 and b == 1:
                wait_load(low_0, 5)
            if k == 0 and b == 2:
                wait_load(diag_b, 8)
                invert(0, [2, 3])
            rows, last = pl.ds(b * CH, CH), pl.ds(B - CH, CH)
            if k == 0:
                part = state[local[0], rows, :]
            else:
                part = work[rows, :] - dot(panel_0[local[1], rows, last], solved[0, last, :])
            for a in range(b):
                if k == 0:
                    tile = low_0[local[0], pl.ds(strip_at[a] + (b - a - 1) * CH, CH), :]
                else:
                    tile = panel_1[local[1], pl.ds(b * CH, CH), pl.ds(a * CH, CH)]
                part = part - (dot(tile, his[a]) + dot(tile, los[a]))
            hi, lo = split(part)
            ihi, ilo = inv_hi[b], inv_lo[b]
            x = dot(ihi, hi) + (dot(ihi, lo) + dot(ilo, hi))
            hi, lo = split(x)
            his.append(hi)
            los.append(lo)
            masked = jnp.where(mine[k], x, 0.0).astype(BF16)
            x_send[k, pl.ds(b * CH, CH), :] = masked
            if k == 0 and b == 0:
                pl.semaphore_wait(barrier, len(peers))
            for dy, flip in around:
                send(x_send.at[k, near_rows(b, dy, flip)], near_recv.at[k, b, dy * 2 + flip], k, b, 0, near(b, dy, flip))

    def arrived(ref, k, c, stage):
        pltpu.make_async_copy(ref, ref, recv_sem.at[k, c, stage]).wait()

    def reduce_near(k, c):
        arrived(near_recv.at[k, c, pl.ds(1, 7)], k, c, 0)
        total = x_send[k, near_rows(c, 0, 0), :]
        for d in range(1, 8):
            total = total + near_recv[k, c, d]
        z_send[k, c] = total
        for d, peer in zip(along, z_peers):
            send(z_send.at[k, c], z_recv.at[k, c, d // 2], k, c, 1, peer)

    def reduce_along(k, c):
        arrived(z_recv.at[k, c, pl.ds(1, 3)], k, c, 1)
        total = (z_send[k, c] + z_recv[k, c, 1]) + (z_recv[k, c, 2] + z_recv[k, c, 3])
        mine_here = near_rows(c, 0, 0)
        solved[k, mine_here, :] = total
        piece = solved.at[k, mine_here]
        for dy, flip in around:
            send(piece, piece, k, c, 2, near(c, dy, flip))

    def gather(k, c):
        arrived(near_recv.at[k, c, pl.ds(1, 7)], k, c, 2)

    wait_load(diag_a, 0)
    invert(0, [0, 1])
    wait_load(state, 1)
    solve(0)
    load_column(0, 2)
    load_diag(1, range(NCH), diag_1, 3)
    load_column(1, 4)
    pltpu.make_async_copy(target_hbm, target_ref, load_sem.at[7]).wait()
    tgt[col, 0:2, :] = target_ref[...]
    for peer in c_peers:
        pltpu.make_async_remote_copy(
            src_ref=tgt.at[col], dst_ref=tgt.at[col], send_sem=tgt_send, recv_sem=tgt_recv,
            device_id=peer, device_id_type=MESH,
        ).start()
    for c in range(NCH):
        reduce_near(0, c)
    for c in range(NCH):
        reduce_along(0, c)
    wait_load(diag_1, 3)
    invert(1, range(NCH))
    work[...] = state[local[1]]
    wait_load(panel_0, 2)
    wait_load(panel_1, 4)
    for c in range(NCH):
        gather(0, c)
        if c == NCH - 1:
            break
        work[...] = work[...] - dot(panel_0[local[1], :, pl.ds(c * CH, CH)], solved[0, pl.ds(c * CH, CH), :])
    solve(1)

    def apply_first(t):
        state[t] = state[t] - dot(panel_0[t], solved[0])

    def apply_second(t, c):
        part = pl.ds(c * CH, CH)
        state[t] = state[t] - dot(panel_1[t, :, part], solved[1, part, :])

    def mean_weights():
        rest = jnp.concatenate([tgt[d] for d in range(NC)], axis=1)
        parts = []
        for _ in range(3):
            parts.append(rest.astype(BF16).astype(F32))
            rest = rest - parts[-1]
        return jnp.concatenate(parts + [jnp.zeros_like(rest)], axis=0).astype(BF16)

    def mean_terms(weights, k):
        found = dot(weights, solved[k])
        return found[k : k + 1] + found[8 + k : 9 + k] + found[16 + k : 17 + k]

    apply_first(0)
    apply_first(1)
    for c in range(NCH):
        reduce_near(1, c)
    apply_first(2)
    for c in range(NCH):
        reduce_along(1, c)
    apply_first(3)
    pltpu.make_async_copy(tgt.at[pl.ds(0, NC - 1)], tgt.at[pl.ds(0, NC - 1)], tgt_recv).wait()
    weights = mean_weights()
    mean = mean_terms(weights, 0)
    done[0] = solved[0]
    kind = jnp.zeros((8, 128), jnp.int32)
    for t in range(blocks):
        here = [(slot_ref[i] == row * blocks + t).astype(jnp.int32) for i in range(2)]
        kind = jnp.where(iota((8, 128), 0) == t, 2 * here[0] + here[1], kind)
    code[...] = kind
    for c in range(NCH):
        gather(1, c)
        done[1, pl.ds(c * CH, CH), :] = solved[1, pl.ds(c * CH, CH), :]
        if c < NCH - 1:
            for t in range(blocks):
                apply_second(t, c)
    mean_ref[...] = (mean + mean_terms(weights, 1)).reshape(W)

    for k in range(2):
        for c in range(NCH):
            for stage, sent in enumerate((near_recv.at[k, c, pl.ds(1, 7)], z_recv.at[k, c, pl.ds(1, 3)], near_recv.at[k, c, pl.ds(1, 7)])):
                pltpu.make_async_copy(sent, sent, send_sem.at[k, c, stage]).wait()
    pltpu.make_async_copy(tgt.at[pl.ds(0, NC - 1)], tgt.at[pl.ds(0, NC - 1)], tgt_send).wait()


def finish(state, panel_1, done, mean, code, out_hbm, mean_hbm, stage, store_sem, mean_sem):
    blocks, rows = 4, B // 2
    last = pl.ds(B - CH, CH)
    pltpu.make_async_copy(mean, mean_hbm, mean_sem).start()
    for t in range(blocks):
        kind = jnp.broadcast_to(code[t : t + 1, :], (rows, 128))
        kind = jnp.concatenate([kind, kind], axis=1)
        for i in range(2):
            part = pl.ds(i * rows, rows)
            value = state[t, part, :] - dot(panel_1[t, part, last], done[1, last, :])
            value = jnp.where(kind == 1, done[1, part, :].astype(F32), value)
            stage[t, part, :] = jnp.where(kind == 2, done[0, part, :].astype(F32), value)
            pltpu.make_async_copy(
                stage.at[t, part], out_hbm.at[pl.ds(t * B + i * rows, rows)], store_sem.at[t, i]
            ).start()
    for t in range(blocks):
        for i in range(2):
            part = pl.ds(i * rows, rows)
            pltpu.make_async_copy(
                stage.at[t, part], out_hbm.at[pl.ds(t * B + i * rows, rows)], store_sem.at[t, i]
            ).wait()
    pltpu.make_async_copy(mean, mean_hbm, mean_sem).wait()


def per_device(panel, rhs, block_slot, target):
    rows, width = rhs.shape
    piece = (PIECE, W)
    held = pl.pallas_call(
        kernel,
        out_shape=(
            pltpu.VMEM((rows // B, B, width), F32),
            pltpu.VMEM((4, B, B), BF16),
            pltpu.VMEM((2, B, W), BF16),
            pltpu.VMEM((width,), F32),
            pltpu.VMEM((8, 128), jnp.int32),
        ),
        in_specs=[pl.BlockSpec(memory_space=pl.ANY)] * 4,
        out_specs=(pl.BlockSpec(memory_space=pltpu.VMEM),) * 5,
        scratch_shapes=[
            pltpu.SMEM((128,), jnp.int32),
            pltpu.VMEM((2, 128), F32),
            pltpu.VMEM((128, BASE * 128), BF16),
            pltpu.VMEM((4, B, B), BF16),
            pltpu.VMEM((4, 6 * CH, CH), BF16),
            pltpu.VMEM((4, 2 * CH, CH), BF16),
            pltpu.VMEM((4, 2 * CH, CH), BF16),
            pltpu.VMEM((4, B, CH), BF16),
            pltpu.VMEM((B, W), F32),
            pltpu.VMEM((NCH, CH, CH), BF16),
            pltpu.VMEM((NCH, CH, CH), BF16),
            pltpu.VMEM((2, B, W), BF16),
            pltpu.VMEM((2, B, W), BF16),
            pltpu.VMEM((2, NCH, 8) + piece, BF16),
            pltpu.VMEM((2, NCH) + piece, BF16),
            pltpu.VMEM((2, NCH, 4) + piece, BF16),
            pltpu.VMEM((NC, 8, 128), F32),
            pltpu.SemaphoreType.DMA((9,)),
            pltpu.SemaphoreType.DMA((2, NCH, 3)),
            pltpu.SemaphoreType.DMA((2, NCH, 3)),
            pltpu.SemaphoreType.DMA,
            pltpu.SemaphoreType.DMA,
        ],
        compiler_params=pltpu.CompilerParams(
            collective_id=0, has_side_effects=True, vmem_limit_bytes=44 * 2**20
        ),
        name="substitute",
    )(block_slot, target, panel, rhs)
    held = [pltpu.with_memory_space_constraint(v, pltpu.VMEM) for v in held]
    return pl.pallas_call(
        finish,
        out_shape=(jax.ShapeDtypeStruct((rows, width), F32), jax.ShapeDtypeStruct((width,), F32)),
        in_specs=[pl.BlockSpec(memory_space=pltpu.VMEM)] * 5,
        out_specs=(pl.BlockSpec(memory_space=pl.ANY),) * 2,
        scratch_shapes=[pltpu.VMEM((4, B, W), F32), pltpu.SemaphoreType.DMA((4, 2)), pltpu.SemaphoreType.DMA],
        compiler_params=pltpu.CompilerParams(vmem_limit_bytes=20 * 2**20),
        name="finish",
    )(*held)


def solution(mesh):
    return jax.shard_map(
        per_device,
        mesh=mesh,
        in_specs=(P("row", None), P("row", "col"), P(), P(None, "col")),
        out_specs=(P("row", "col"), P("col")),
        check_vma=False,
    )
```
